256 devices in a mesh: dp: 64 (over z, y, core), seq: 4 (over x).
Axes of the slice: x: 4, y: 4, z: 8, core: 2. Of those that a mesh axis runs over, the one named last changes fastest.
Arguments:
- queries: bfloat16 [32768, 3072], P(('dp', 'seq')), may hold values from -6 to 6
- keys: bfloat16 [32768, 3072], P(('dp', 'seq')), may hold values from -6 to 6
- values: bfloat16 [32768, 3072], P(('dp', 'seq')), may hold values from -6 to 6
- upstream: bfloat16 [32768, 3072], P(('dp', 'seq')), may hold values from -6 to 6
- dest_group: int32 [32768, 1], replicated, may hold values from 0 to 63; in each aligned block of 128 rows (0 to 127, 128 to 255, ...) at most 3 rows name the same one
- clip_ids: int32 [32768], replicated, may hold values from 0 to 2
Outputs:
- attended: bfloat16 [32768, 3072], P(('dp', 'seq'))
- grad_query: bfloat16 [32768, 3072], P(('dp', 'seq'))
- grad_key: bfloat16 [32768, 3072], P(('dp', 'seq'))
- grad_value: bfloat16 [32768, 3072], P(('dp', 'seq'))
The draws below stay inside these ranges and needn't reach their ends.
Inputs may be any that keep to these rules, and one draw needn't show every extreme that they name: `dest_group`: among the rows of one device (aligned blocks of 128 rows) no data group is named more than 3 times; in every draw some device names some group exactly 3 times.
All inputs are finite; a program needn't handle non-finite values.
Results may differ from the reference program's by a relative error of at most 0.024.
Values may be sent and summed in bfloat16 or wider, within the bound.
No kernel may reach another device: no remote copies, remote signals or barrier semaphores. Data moves between devices by JAX's collectives and lax.ppermute only.
A program may use at most 128 MiB of HBM per device.

```python
import math
import jax
import jax.numpy as jnp
import numpy as np
from jax import lax

HEADS = 24
HD = 128
TOK_DEV = 128
CLIPS = 3
CAP = 3
ROWS = 32768
N_DP = 64
N_SEQ = 4


def shared_keys(key):
    base = jax.random.fold_in(key, 101)
    raw_keys = jax.random.normal(jax.random.fold_in(base, 1), (ROWS, HEADS * HD), jnp.float32)
    return raw_keys


def draw_keys(key, part):
    raw_keys = shared_keys(key)
    result = jnp.clip(raw_keys, -6.0, 6.0)
    return result.astype(jnp.bfloat16)


def draw_queries(key, part):
    key = jax.random.fold_in(key, 13)
    result = jnp.clip(jax.random.normal(key, (ROWS, HEADS * HD), jnp.float32), -6.0, 6.0)
    return result.astype(jnp.bfloat16)


def plant(entries, key, smallest, top_value):
    extent = entries.shape
    spot = [jax.random.randint(jax.random.fold_in(key, axis), (), 0, extent[axis]) for axis in range(len(extent))]
    entries = entries.at[tuple(spot)].set(smallest)
    longest = extent.index(max(extent))
    spot[longest] = (spot[longest] + 1) % extent[longest]
    return entries.at[tuple(spot)].set(top_value)


def block_levels(own_key, extent, split, least, top_value):
    def one(position, shards_of):
        steps = jax.random.uniform(jax.random.fold_in(jax.random.fold_in(own_key, 6), position), (shards_of,), jnp.float32, least / len(split), top_value / len(split))
        return jnp.repeat(jnp.exp(steps), extent[position] // shards_of).reshape((-1,) + (1,) * (len(extent) - position - 1))

    level = one(*split[0])
    for cut in split[1:]:
        level = level * one(*cut)
    return level


def rank_table(count, slope):
    weights = [(1 << 20) // math.isqrt(rank ** slope) + 1 for rank in range(1, count + 1)]
    width = 1 + sum(weights) // (1 << 30)
    return np.cumsum(np.array([max(1, weight // width) for weight in weights]))


def ranked(own_key, dims, count, slope):
    listing = rank_table(count, slope)
    pick = jax.random.randint(jax.random.fold_in(own_key, 1), dims, 0, int(listing[count - 1]))
    standing = jnp.searchsorted(jnp.asarray(listing, jnp.int32), pick, side="right")
    return jax.random.permutation(jax.random.fold_in(own_key, 2), count)[standing].astype(jnp.int32)


def routed_block(rng, own, number, rows, number_of, top, most, skew):
    order = jax.random.permutation(rng, number_of)
    crowded, usual = portions_of(number_of, rows * top, most, skew, True), portions_of(number_of, rows * top, most, skew, False)
    places = jnp.arange(number_of)

    def named(lengths, offset_by):
        used = int((lengths > 0).sum())
        fixed = max(1, used // 4)
        shifted = fixed + (places - fixed + offset_by * (used - fixed)) % max(1, number_of - fixed)
        return jnp.zeros((number_of,), jnp.int32).at[order[jnp.where(places < fixed, places, shifted)]].set(jnp.asarray(lengths, jnp.int32))

    lengths = jnp.where(number % 4 == 0, named(crowded, number // 4), named(usual, number - number // 4 - 1))
    mixed = jax.random.permutation(jax.random.fold_in(own, 3), number_of)
    donor, sink = mixed[0:number_of // 2 * 2:2], mixed[1:number_of // 2 * 2:2]
    margin = jnp.minimum(lengths[donor] - 1, most - lengths[sink]) // 2
    margin = jnp.where((donor == order[0]) | (sink == order[0]) | (lengths[sink] == 0), 0, jnp.maximum(margin, 0))
    shifted = jax.random.randint(jax.random.fold_in(own, 4), (number_of // 2,), 0, 1 << 20) % (margin + 1)
    lengths = lengths.at[donor].add(-shifted).at[sink].add(shifted)
    members = jnp.searchsorted(jnp.cumsum(lengths), jnp.arange(rows * top), side="right").astype(jnp.int32)
    listing = members.reshape(top, rows).T
    listing = listing[jax.random.permutation(jax.random.fold_in(own, 1), rows)]
    offset_by = jax.random.randint(jax.random.fold_in(own, 2), (rows, 1), 0, top)
    return jnp.take_along_axis(listing, (jnp.arange(top)[None, :] + offset_by) % top, axis=1)


def portions_of(count, total, bound, skew, full):
    portions = [(1 << 20) // math.isqrt(rank ** skew) + 1 for rank in range(1, count + 1)]
    largest = bound if full else min(bound, max(-(-total // count), total * portions[0] // sum(portions)))
    least = 1 if total - largest >= count - 1 else 0
    counts, spare = [largest] + [least] * (count - 1), total - largest - least * (count - 1)
    while spare > 0:
        movable = [i for i in range(1, count) if counts[i] < largest] or [i for i in range(1, count) if counts[i] < bound]
        pool, left = sum([portions[i] for i in movable]), spare
        for i in movable:
            more = min(bound - counts[i], max(1, left * portions[i] // pool), spare)
            counts[i] = counts[i] + more
            spare = spare - more
    return np.array(counts)


def bell_draw(stream_key, extent, scale, bound, pieces=(), held_as=jnp.bfloat16):
    values = scale * jax.random.normal(stream_key, extent, jnp.float32)
    if pieces:
        values = values * block_levels(stream_key, extent, pieces, -0.22, 0.18)
    return jnp.clip(values, -bound, bound).astype(held_as)


def setup_inputs(seed: int = 0) -> dict:
    arg_keys = jax.random.split(jax.random.key(seed), 7)
    queries = draw_queries(jax.random.fold_in(arg_keys[6], 71), 0)
    keys = draw_keys(jax.random.fold_in(arg_keys[6], 71), 0)
    values = bell_draw(arg_keys[2], (ROWS, HEADS * HD), 1.0, 6.0, ((0, 256),))
    upstream = bell_draw(arg_keys[3], (ROWS, HEADS * HD), 1.0, 6.0, ((0, 256),))
    dest_group_keys = jax.random.split(jax.random.fold_in(arg_keys[4], 1), ROWS // TOK_DEV)
    dest_group_turns = jax.random.permutation(jax.random.fold_in(arg_keys[4], 3), ROWS // TOK_DEV)
    dest_group = jax.vmap(lambda own, number: routed_block(jax.random.fold_in(arg_keys[4], 2), own, number, TOK_DEV, N_DP, 1, CAP, 2))(dest_group_keys, dest_group_turns).reshape((ROWS, 1))
    clip_ids = plant(ranked(arg_keys[5], (ROWS,), CLIPS, 2), jax.random.fold_in(arg_keys[5], 3), 0, CLIPS - 1).astype(jnp.int32)
    return {"queries": queries, "keys": keys, "values": values, "upstream": upstream, "dest_group": dest_group, "clip_ids": clip_ids}


def reference(queries, keys, values, upstream, dest_group, clip_ids):
    row_count = queries.shape[0]
    devices = N_DP * N_SEQ
    span = N_SEQ * N_DP * CAP
    scale = HD ** -0.5
    targets = dest_group[:, 0].reshape(devices, TOK_DEV)
    earlier = lax.broadcasted_iota(jnp.int32, (TOK_DEV, TOK_DEV), 1) < lax.broadcasted_iota(jnp.int32, (TOK_DEV, TOK_DEV), 0)
    matching = targets[:, :, None] == targets[:, None, :]
    row_ranks = jnp.sum((matching & earlier[None]).astype(jnp.int32), axis=2)
    device_ids = jnp.arange(devices, dtype=jnp.int32)[:, None]
    slot_place = (device_ids % N_SEQ) * (N_DP * CAP) + (device_ids // N_SEQ) * CAP + row_ranks
    row_ids = jnp.arange(row_count, dtype=jnp.int32)
    slot_table = jnp.full((N_DP, span), row_count, jnp.int32)
    slot_table = slot_table.at[targets.reshape(-1), slot_place.reshape(-1)].set(row_ids)
    identity = lax.broadcasted_iota(jnp.int32, (span, span), 0) == lax.broadcasted_iota(jnp.int32, (span, span), 1)

    def one_group(carry, group_index):
        index = lax.dynamic_index_in_dim(slot_table, group_index, 0, keepdims=False)
        valid = index < row_count
        safe = jnp.minimum(index, row_count - 1)
        labels = jnp.where(valid, clip_ids[safe] + 1, 0)
        related = ((labels[:, None] == labels[None, :]) & (labels[:, None] > 0)) | identity
        query_rows = queries[safe].astype(jnp.float32).reshape(span, HEADS, HD)
        key_rows = keys[safe].astype(jnp.float32).reshape(span, HEADS, HD)
        value_rows = values[safe].astype(jnp.float32).reshape(span, HEADS, HD)
        upstream_rows = upstream[safe].astype(jnp.float32).reshape(span, HEADS, HD)
        scores = jnp.einsum("qhd,khd->hqk", query_rows, key_rows) * scale
        scores = jnp.where(related[None], scores, -1e30)
        row_max = jnp.max(scores, axis=2, keepdims=True)
        weights = jnp.where(related[None], jnp.exp(scores - row_max), 0.0)
        probs = weights / jnp.sum(weights, axis=2, keepdims=True)
        probs_b = probs.astype(jnp.bfloat16)
        attended = jnp.einsum("hqk,khd->qhd", probs_b.astype(jnp.float32), value_rows).astype(jnp.bfloat16)
        delta = jnp.sum(upstream_rows * attended.astype(jnp.float32), axis=2)
        dprobs = jnp.einsum("qhd,khd->hqk", upstream_rows, value_rows)
        dscores = (probs * (dprobs - jnp.transpose(delta)[:, :, None])).astype(jnp.bfloat16)
        dscores_f = dscores.astype(jnp.float32)
        grad_query = (jnp.einsum("hqk,khd->qhd", dscores_f, key_rows) * scale).astype(jnp.bfloat16)
        grad_key = (jnp.einsum("hqk,qhd->khd", dscores_f, query_rows) * scale).astype(jnp.bfloat16)
        grad_value = jnp.einsum("hqk,qhd->khd", probs_b.astype(jnp.float32), upstream_rows).astype(jnp.bfloat16)
        results = (attended, grad_query, grad_key, grad_value)
        updated = tuple(
            whole.at[index].set(part_rows.reshape(span, HEADS * HD), mode="drop")
            for whole, part_rows in zip(carry, results)
        )
        return updated, None

    start = tuple(jnp.zeros((row_count, HEADS * HD), jnp.bfloat16) for _ in range(4))
    final, _ = lax.scan(one_group, start, jnp.arange(N_DP, dtype=jnp.int32))
    return (final[0], final[1], final[2], final[3])
```

```python
import jax
import jax.numpy as jnp
from jax import lax
from jax.sharding import PartitionSpec as P

HD = 128


def prior_count(targets):
    length = targets.shape[-1]
    earlier = lax.broadcasted_iota(jnp.int32, (length, length), 1) < lax.broadcasted_iota(
        jnp.int32, (length, length), 0
    )
    matching = targets[..., :, None] == targets[..., None, :]
    return jnp.sum((matching & earlier).astype(jnp.int32), axis=-1)


def slot_labels(targets, clip_table, group_index, capacity):
    arriving = targets == group_index
    row_ranks = prior_count(targets)
    slot_ids = lax.broadcasted_iota(jnp.int32, (capacity,), 0)
    filled = arriving[:, None, :] & (row_ranks[:, None, :] == slot_ids[None, :, None])
    return jnp.sum(jnp.where(filled, clip_table[:, None, :] + 1, 0), axis=-1)


def return_rows(positions, slot_count, stacked):
    picker = (
        positions[:, None] == lax.broadcasted_iota(jnp.int32, (positions.shape[0], slot_count), 1)
    ).astype(jnp.bfloat16)
    return jnp.einsum("ts,nsc->ntc", picker, stacked, preferred_element_type=jnp.float32).astype(
        jnp.bfloat16
    )


def attend_forward(query_rows, key_rows, value_rows, related):
    scale = HD ** (-0.5)
    contract_cols = (((1,), (1,)), ((), ()))
    prob_list, probs_b_list, out_list = ([], [], [])
    for head_index in range(query_rows.shape[1] // HD):
        lower = head_index * HD
        query_head = query_rows[:, lower : lower + HD]
        key_head = key_rows[:, lower : lower + HD]
        value_head = value_rows[:, lower : lower + HD]
        scores = (
            lax.dot_general(query_head, key_head, contract_cols, preferred_element_type=jnp.float32)
            * scale
        )
        scores = jnp.where(related, scores, -1e30)
        row_max = jnp.max(scores, axis=1, keepdims=True)
        weights = jnp.where(related, jnp.exp(scores - row_max), 0.0)
        probs = weights / jnp.sum(weights, axis=1, keepdims=True)
        probs_b = probs.astype(jnp.bfloat16)
        prob_list.append(probs)
        probs_b_list.append(probs_b)
        out_list.append(
            jnp.dot(probs_b, value_head, preferred_element_type=jnp.float32).astype(jnp.bfloat16)
        )
    return (prob_list, probs_b_list, jnp.concatenate(out_list, axis=1))


def attend_backward(
    query_rows, key_rows, value_rows, upstream_rows, attended, prob_list, probs_b_list
):
    scale = HD ** (-0.5)
    contract_cols = (((1,), (1,)), ((), ()))
    contract_rows = (((0,), (0,)), ((), ()))
    query_grads, key_grads, value_grads = ([], [], [])
    for head_index in range(query_rows.shape[1] // HD):
        lower = head_index * HD
        query_head = query_rows[:, lower : lower + HD]
        key_head = key_rows[:, lower : lower + HD]
        value_head = value_rows[:, lower : lower + HD]
        upstream_head = upstream_rows[:, lower : lower + HD]
        out_head = attended[:, lower : lower + HD]
        delta = jnp.sum(
            upstream_head.astype(jnp.float32) * out_head.astype(jnp.float32), axis=1, keepdims=True
        )
        dprobs = lax.dot_general(
            upstream_head, value_head, contract_cols, preferred_element_type=jnp.float32
        )
        dscores = (prob_list[head_index] * (dprobs - delta)).astype(jnp.bfloat16)
        query_grads.append(
            (jnp.dot(dscores, key_head, preferred_element_type=jnp.float32) * scale).astype(
                jnp.bfloat16
            )
        )
        key_grads.append(
            (
                lax.dot_general(
                    dscores, query_head, contract_rows, preferred_element_type=jnp.float32
                )
                * scale
            ).astype(jnp.bfloat16)
        )
        value_grads.append(
            lax.dot_general(
                probs_b_list[head_index],
                upstream_head,
                contract_rows,
                preferred_element_type=jnp.float32,
            ).astype(jnp.bfloat16)
        )
    return (
        jnp.concatenate(query_grads, axis=1),
        jnp.concatenate(key_grads, axis=1),
        jnp.concatenate(value_grads, axis=1),
    )


def body(queries, keys, values, upstream, dest_group, clip_ids):
    group_count = lax.axis_size("dp")
    part_count = lax.axis_size("seq")
    group_index = lax.axis_index("dp")
    seq_index = lax.axis_index("seq")
    row_count = queries.shape[0]
    capacity = (3 * row_count + 2 * group_count - 1) // (2 * group_count)
    targets = dest_group[:, 0].reshape(group_count, part_count, row_count)
    clip_table = clip_ids.reshape(group_count, part_count, row_count)
    label_table = slot_labels(
        targets.reshape(group_count * part_count, row_count),
        clip_table.reshape(group_count * part_count, row_count),
        group_index,
        capacity,
    ).reshape(group_count, part_count, capacity)
    own_group = lax.dynamic_index_in_dim(targets, group_index, 0, keepdims=False)
    labels = label_table.reshape(-1)
    own_rows = lax.dynamic_index_in_dim(own_group, seq_index, 0, keepdims=False)
    positions = own_rows * capacity + prior_count(own_rows)
    slots = group_count * capacity
    picker = (
        lax.broadcasted_iota(jnp.int32, (slots, row_count), 0) == positions[None, :]
    ).astype(jnp.bfloat16)
    width = queries.shape[1] // part_count
    stacked = jnp.stack((queries, keys, values, upstream))
    packed = jnp.einsum("st,ntc->snc", picker, stacked, preferred_element_type=jnp.float32).astype(
        jnp.bfloat16
    )
    blocks = packed.reshape(group_count, capacity, 4, part_count, width)
    blocks = jnp.transpose(blocks, (0, 3, 1, 2, 4)).reshape(-1, capacity, 4, width)
    arrived = lax.all_to_all(blocks, ("dp", "seq"), split_axis=0, concat_axis=0, tiled=True)
    regrouped = jnp.transpose(arrived, (2, 0, 1, 3)).reshape(4, -1, width)
    slot_total = labels.shape[0]
    identity = lax.broadcasted_iota(jnp.int32, (slot_total, slot_total), 0) == lax.broadcasted_iota(
        jnp.int32, (slot_total, slot_total), 1
    )
    related = (labels[:, None] == labels[None, :]) & (labels[:, None] > 0) | identity
    prob_list, probs_b_list, attended = attend_forward(
        regrouped[0], regrouped[1], regrouped[2], related
    )
    gradients = attend_backward(
        regrouped[0], regrouped[1], regrouped[2], regrouped[3], attended, prob_list, probs_b_list
    )
    results = jnp.stack((attended, gradients[0], gradients[1], gradients[2]), axis=1)
    results = results.reshape(-1, capacity, 4, width)
    routed_back = lax.all_to_all(results, ("dp", "seq"), split_axis=0, concat_axis=0, tiled=True)
    routed_back = routed_back.reshape(group_count, part_count, capacity, 4, width)
    routed_back = jnp.transpose(routed_back, (3, 0, 2, 1, 4)).reshape(4, slots, -1)
    all_home = return_rows(positions, slots, routed_back)
    return (all_home[0], all_home[1], all_home[2], all_home[3])


def solution(mesh):
    return jax.shard_map(
        body,
        mesh=mesh,
        in_specs=(
            P(("dp", "seq"), None),
            P(("dp", "seq"), None),
            P(("dp", "seq"), None),
            P(("dp", "seq"), None),
            P(),
            P(),
        ),
        out_specs=(
            P(("dp", "seq"), None),
            P(("dp", "seq"), None),
            P(("dp", "seq"), None),
            P(("dp", "seq"), None),
        ),
        check_vma=False,
    )
```

```python
import jax
import jax.numpy as jnp
from jax import lax
from jax.experimental import pallas as pl
from jax.experimental.pallas import tpu as pltpu
from jax.sharding import PartitionSpec as P

HD = 128


def prior_count(targets):
    length = targets.shape[-1]
    earlier = lax.broadcasted_iota(jnp.int32, (length, length), 1) < lax.broadcasted_iota(
        jnp.int32, (length, length), 0
    )
    matching = targets[..., :, None] == targets[..., None, :]
    return jnp.sum((matching & earlier).astype(jnp.int32), axis=-1)


def slot_labels(targets, clip_table, group_index, capacity):
    arriving = targets == group_index
    row_ranks = prior_count(targets)
    slot_ids = lax.broadcasted_iota(jnp.int32, (capacity,), 0)
    filled = arriving[:, None, :] & (row_ranks[:, None, :] == slot_ids[None, :, None])
    return jnp.sum(jnp.where(filled, clip_table[:, None, :] + 1, 0), axis=-1)


def return_rows(positions, slot_count, stacked):
    picker = (
        positions[:, None] == lax.broadcasted_iota(jnp.int32, (positions.shape[0], slot_count), 1)
    ).astype(jnp.bfloat16)
    return jnp.einsum("ts,nsc->ntc", picker, stacked, preferred_element_type=jnp.float32).astype(
        jnp.bfloat16
    )


def attend_forward(query_rows, key_rows, value_rows, related):
    scale = HD ** (-0.5)
    contract_cols = (((1,), (1,)), ((), ()))
    prob_list, probs_b_list, out_list = ([], [], [])
    for head_index in range(query_rows.shape[1] // HD):
        lower = head_index * HD
        query_head = query_rows[:, lower : lower + HD]
        key_head = key_rows[:, lower : lower + HD]
        value_head = value_rows[:, lower : lower + HD]
        scores = (
            lax.dot_general(query_head, key_head, contract_cols, preferred_element_type=jnp.float32)
            * scale
        )
        scores = jnp.where(related, scores, -1e30)
        row_max = jnp.max(scores, axis=1, keepdims=True)
        weights = jnp.where(related, jnp.exp(scores - row_max), 0.0)
        probs = weights / jnp.sum(weights, axis=1, keepdims=True)
        probs_b = probs.astype(jnp.bfloat16)
        prob_list.append(probs)
        probs_b_list.append(probs_b)
        out_list.append(
            jnp.dot(probs_b, value_head, preferred_element_type=jnp.float32).astype(jnp.bfloat16)
        )
    return (prob_list, probs_b_list, jnp.concatenate(out_list, axis=1))


def attend_backward(
    query_rows, key_rows, value_rows, upstream_rows, attended, prob_list, probs_b_list
):
    scale = HD ** (-0.5)
    contract_cols = (((1,), (1,)), ((), ()))
    contract_rows = (((0,), (0,)), ((), ()))
    query_grads, key_grads, value_grads = ([], [], [])
    for head_index in range(query_rows.shape[1] // HD):
        lower = head_index * HD
        query_head = query_rows[:, lower : lower + HD]
        key_head = key_rows[:, lower : lower + HD]
        value_head = value_rows[:, lower : lower + HD]
        upstream_head = upstream_rows[:, lower : lower + HD]
        out_head = attended[:, lower : lower + HD]
        delta = jnp.sum(
            upstream_head.astype(jnp.float32) * out_head.astype(jnp.float32), axis=1, keepdims=True
        )
        dprobs = lax.dot_general(
            upstream_head, value_head, contract_cols, preferred_element_type=jnp.float32
        )
        dscores = (prob_list[head_index] * (dprobs - delta)).astype(jnp.bfloat16)
        query_grads.append(
            (jnp.dot(dscores, key_head, preferred_element_type=jnp.float32) * scale).astype(
                jnp.bfloat16
            )
        )
        key_grads.append(
            (
                lax.dot_general(
                    dscores, query_head, contract_rows, preferred_element_type=jnp.float32
                )
                * scale
            ).astype(jnp.bfloat16)
        )
        value_grads.append(
            lax.dot_general(
                probs_b_list[head_index],
                upstream_head,
                contract_rows,
                preferred_element_type=jnp.float32,
            ).astype(jnp.bfloat16)
        )
    return (
        jnp.concatenate(query_grads, axis=1),
        jnp.concatenate(key_grads, axis=1),
        jnp.concatenate(value_grads, axis=1),
    )


def plain_path(queries, keys, values, upstream, dest_group, clip_ids):
    group_count = lax.axis_size("dp")
    part_count = lax.axis_size("seq")
    group_index = lax.axis_index("dp")
    seq_index = lax.axis_index("seq")
    row_count = queries.shape[0]
    capacity = (3 * row_count + 2 * group_count - 1) // (2 * group_count)
    targets = dest_group[:, 0].reshape(group_count, part_count, row_count)
    clip_table = clip_ids.reshape(group_count, part_count, row_count)
    label_table = slot_labels(
        targets.reshape(group_count * part_count, row_count),
        clip_table.reshape(group_count * part_count, row_count),
        group_index,
        capacity,
    ).reshape(group_count, part_count, capacity)
    own_group = lax.dynamic_index_in_dim(targets, group_index, 0, keepdims=False)
    labels = label_table.reshape(-1)
    own_rows = lax.dynamic_index_in_dim(own_group, seq_index, 0, keepdims=False)
    positions = own_rows * capacity + prior_count(own_rows)
    slots = group_count * capacity
    picker = (
        lax.broadcasted_iota(jnp.int32, (slots, row_count), 0) == positions[None, :]
    ).astype(jnp.bfloat16)
    width = queries.shape[1] // part_count
    stacked = jnp.stack((queries, keys, values, upstream))
    packed = jnp.einsum("st,ntc->snc", picker, stacked, preferred_element_type=jnp.float32).astype(
        jnp.bfloat16
    )
    blocks = packed.reshape(group_count, capacity, 4, part_count, width)
    blocks = jnp.transpose(blocks, (0, 3, 1, 2, 4)).reshape(-1, capacity, 4, width)
    arrived = lax.all_to_all(blocks, ("dp", "seq"), split_axis=0, concat_axis=0, tiled=True)
    regrouped = jnp.transpose(arrived, (2, 0, 1, 3)).reshape(4, -1, width)
    slot_total = labels.shape[0]
    identity = lax.broadcasted_iota(jnp.int32, (slot_total, slot_total), 0) == lax.broadcasted_iota(
        jnp.int32, (slot_total, slot_total), 1
    )
    related = (labels[:, None] == labels[None, :]) & (labels[:, None] > 0) | identity
    prob_list, probs_b_list, attended = attend_forward(
        regrouped[0], regrouped[1], regrouped[2], related
    )
    gradients = attend_backward(
        regrouped[0], regrouped[1], regrouped[2], regrouped[3], attended, prob_list, probs_b_list
    )
    results = jnp.stack((attended, gradients[0], gradients[1], gradients[2]), axis=1)
    results = results.reshape(-1, capacity, 4, width)
    routed_back = lax.all_to_all(results, ("dp", "seq"), split_axis=0, concat_axis=0, tiled=True)
    routed_back = routed_back.reshape(group_count, part_count, capacity, 4, width)
    routed_back = jnp.transpose(routed_back, (3, 0, 2, 1, 4)).reshape(4, slots, -1)
    all_home = return_rows(positions, slots, routed_back)
    return (all_home[0], all_home[1], all_home[2], all_home[3])

PAGES = 14
HEAVY_MAX = 12
SPAN = 256
MIB = 1 << 20
NONE = -1.0
F32 = jnp.float32
BF16 = jnp.bfloat16
PAIRS = (
    (0, ((0, 0),)),
    (1, ((1, 0),)),
    (2, ((2, 0),)),
    (3, ((3, 0),)),
    (4, ((0, 1), (1, 2), (4, 3))),
    (5, ((2, 1), (3, 2), (4, 4), (5, 5))),
    (6, ((4, 6), (5, 7))),
)
CODES = 8


def iota(shape, dim):
    return lax.broadcasted_iota(jnp.int32, shape, dim)


def dot(a, b, dims=(((1,), (0,)), ((), ()))):
    return lax.dot_general(a, b, dims, preferred_element_type=F32)


def page_codes(axis, heavy, heavy_rank):
    shape = (128, 512) if axis == 0 else (512, 128)
    place = iota(shape, 1 - axis)
    index = iota(shape, axis)

    def total(values):
        return jnp.sum(values, axis=axis, keepdims=True).astype(jnp.int32)

    light = (index < 64) & (heavy < 0.5)
    home = place >> 3
    line = iota((1, 512) if axis == 0 else (512, 1), 1 - axis)
    own, second, array = line >> 3, (line >> 2) & 1, line & 3
    is_heavy = total(jnp.where(index == home, heavy, 0.0)) > 0
    below = total(jnp.where(index < home, heavy, 0.0))
    heavies = total(jnp.where(index == index, heavy, 0.0))
    rank = own - below
    index_f = index.astype(F32)
    heavy_rank_i = heavy_rank.astype(jnp.int32)
    served = total(jnp.where((heavy > 0.5) & (heavy_rank_i == (rank >> 1)), index_f, 0.0))
    eased = total(jnp.where(light & (index - heavy_rank_i == rank - 2 * heavies), index_f, 0.0))
    is_light = jnp.logical_not(is_heavy)
    role_a = is_light & (rank < 2 * heavies)
    role_b = is_light & (rank >= 2 * heavies) & (rank < 4 * heavies)
    odd = (rank & 1) == 1
    even = jnp.logical_not(odd)
    not_a = is_light & (rank >= 2 * heavies)
    first = second == 0

    def code(cond, group, slot):
        return jnp.where(cond, 4 * (3 * group + slot) + array, -1)

    codes = (
        4 * (3 * own + second) + array,
        code(is_heavy & first, own, 2),
        code(is_heavy & jnp.logical_not(first), own, 2),
        code(is_light, own, second),
        code(role_a & even, served, second),
        jnp.maximum(code(role_a & odd, served, second), code(not_a, own, second)),
        code(role_a & even & first, served, 2),
        jnp.maximum(code(role_a & odd & first, served, 2), code(role_b, eased, second)),
    )
    return tuple(c.astype(F32) for c in codes)


def pack_kernel(me_ref, targets_ref, q_ref, k_ref, v_ref, u_ref, send_ref, codes_ref, home_ref, info_ref):
    device, group = me_ref[0], me_ref[1]
    targets = targets_ref[...]
    lane = iota((SPAN, 128), 1)
    ones = jnp.ones((128, 128), BF16)
    flags = jnp.zeros((SPAN, 128), jnp.int32)
    shift = 2 * (lane & 7)
    spread = jnp.left_shift(jnp.ones((SPAN, 128), jnp.int32), 2 * (targets & 7))
    for word in range(8):
        bits = jnp.where((targets >> 3) == word, spread, 0).astype(F32).astype(BF16)
        counts = dot(bits, ones).astype(jnp.int32)
        three = jnp.right_shift(counts, shift) & jnp.right_shift(counts, shift + 1) & 1
        flags = jnp.where((lane >> 3) == word, three, flags)
    heavy = jnp.max(flags.astype(F32), axis=0, keepdims=True)
    square = (128, 128)
    row, col = iota(square, 0), iota(square, 1)
    heavy_l = jnp.broadcast_to(heavy, square)
    earlier = jnp.where(row < col, 1.0, 0.0).astype(BF16)
    rank_l = dot(heavy_l.astype(BF16), earlier)
    heavy_c, rank_c = heavy_l.T, rank_l.T
    codes_c = page_codes(1, heavy_l[:1], rank_l[:1])
    codes_l = page_codes(0, heavy_c[:, :1], rank_c[:, :1])
    for n in range(CODES):
        codes_ref[n : n + 1, :] = codes_l[n]

    mine = jnp.broadcast_to(targets_ref[pl.ds(device, 1), :].astype(F32), square)
    mine_c = mine.T
    same = mine == mine_c
    prior_l = jnp.sum(jnp.where(same & (row < col), 1.0, 0.0), axis=0, keepdims=True)
    prior_c = jnp.sum(jnp.where(same & (col < row), 1.0, 0.0), axis=1, keepdims=True)
    key_l = 12.0 * mine[:1] + 4.0 * prior_l
    key_c = 12.0 * mine_c + 4.0 * prior_c
    key_l = jnp.concatenate([key_l + float(a) for a in range(4)], axis=1)
    for a in range(4):
        home_ref[a * 128 : (a + 1) * 128, :] = key_c + float(a)

    def pick(n):
        return jnp.where(codes_c[n] == key_l, 1.0, 0.0).astype(BF16)

    def columns(head):
        return jnp.concatenate(
            [
                jnp.concatenate(
                    [ref[:, (6 * x + head) * HD : (6 * x + head + 1) * HD] for x in range(4)], axis=1
                )
                for ref in (q_ref, k_ref, v_ref, u_ref)
            ],
            axis=0,
        )

    pickers = [pick(n) for n in range(CODES)]
    for pair, parts in PAIRS:
        total = None
        for head, n in parts:
            term = dot(pickers[n], columns(head))
            total = term if total is None else total + term
        for x in range(4):
            tile = total[:, x * 128 : (x + 1) * 128].reshape(64, 8, 128)
            send_ref[:, x, 8 * pair : 8 * pair + 8, :] = tile.astype(BF16)

    lane1 = iota((1, 128), 1)
    heavy1, rank1 = heavy_l[:1], rank_l[:1]

    def scalar(values):
        return jnp.sum(values).astype(jnp.int32)

    heavies = scalar(heavy1)
    is_heavy = scalar(jnp.where(lane1 == group, heavy1, 0.0))
    rank = group - scalar(jnp.where(lane1 < group, heavy1, 0.0))
    lane_f = lane1.astype(F32)
    rank1_i = rank1.astype(jnp.int32)
    served = scalar(jnp.where((heavy1 > 0.5) & (rank1_i == (rank >> 1)), lane_f, 0.0))
    light1 = (heavy1 < 0.5) & (lane1 < 64)
    eased = scalar(jnp.where(light1 & (lane1 - rank1_i == rank - 2 * heavies), lane_f, 0.0))
    role_a = (is_heavy == 0) & (rank < 2 * heavies)
    role_b = (is_heavy == 0) & (rank >= 2 * heavies) & (rank < 4 * heavies)
    info_ref[0] = heavies
    info_ref[1] = jnp.where(is_heavy > 0, 0, jnp.where(role_a, 5, jnp.where(role_b, 7, 6)))
    info_ref[2] = jnp.where(is_heavy > 0, 4, jnp.where(role_a, 1, 0))
    info_ref[3] = jnp.where(role_a, served, jnp.where(role_b, eased, group))
    info_ref[4] = group
    info_ref[5] = is_heavy


def label_kernel(info_ref, targets_ref, clips_ref, col_ref, row_ref):
    targets = targets_ref[...]
    clips = clips_ref[...] + 1
    row, col = iota((128, 128), 0), iota((128, 128), 1)
    earlier = jnp.where(row < col, 1.0, 0.0).astype(BF16)
    ones = jnp.ones((128, 128), BF16)
    for n in range(2):
        arriving = targets == info_ref[4 - n]
        rank = dot(jnp.where(arriving, 1.0, 0.0).astype(BF16), earlier).astype(jnp.int32)
        for slot in range(3):
            labels = jnp.where(arriving & (rank == slot), clips, 0).astype(F32).astype(BF16)
            col_ref[n, slot * SPAN : (slot + 1) * SPAN, :] = dot(labels, ones)
            row_ref[n, :, slot * SPAN : (slot + 1) * SPAN] = dot(
                ones[:8], labels, (((1,), (1,)), ((), ()))
            )


def attend_unit(d_ref, e_ref, col_ref, row_ref, start, third, which, count):
    scale = HD**-0.5
    rows_t = (((1,), (1,)), ((), ()))
    cols_t = (((0,), (0,)), ((), ()))
    places = [start, start + SPAN] + ([third] if count == 3 else [])

    def load(a):
        return jnp.concatenate([d_ref[a, pl.ds(place, SPAN), :] for place in places], axis=0)

    key, value = load(1), load(2)
    row_labels = row_ref[which, 0:1, : count * SPAN]
    grad_key, grad_value = None, None
    for n, place in enumerate(places):
        query = d_ref[0, pl.ds(place, SPAN), :]
        cotangent = d_ref[3, pl.ds(place, SPAN), :]
        labels = col_ref[which, n * SPAN : (n + 1) * SPAN, :]
        related = jnp.concatenate([labels] * (2 * count), axis=1) == row_labels
        scores = jnp.where(related, dot(query, key, rows_t), -1e30)
        top = jnp.max(scores, axis=1, keepdims=True)
        weights = jnp.exp2((scores - top) * (scale * 1.4426950408889634))
        probs = weights * (1.0 / jnp.sum(weights, axis=1, keepdims=True))
        probs_b = probs.astype(BF16)
        attended = dot(probs_b, value).astype(BF16)
        delta = jnp.sum(cotangent.astype(F32) * attended.astype(F32), axis=1, keepdims=True)
        dscores = (probs * (dot(cotangent, value, rows_t) - delta)).astype(BF16)
        e_ref[0, pl.ds(place, SPAN), :] = attended
        e_ref[1, pl.ds(place, SPAN), :] = (dot(dscores, key) * scale).astype(BF16)
        term_key = dot(dscores, query, cols_t)
        term_value = dot(probs_b, cotangent, cols_t)
        grad_key = term_key if n == 0 else grad_key + term_key
        grad_value = term_value if n == 0 else grad_value + term_value
    for n, place in enumerate(places):
        part = slice(n * SPAN, (n + 1) * SPAN)
        e_ref[2, pl.ds(place, SPAN), :] = (grad_key[part] * scale).astype(BF16)
        e_ref[3, pl.ds(place, SPAN), :] = grad_value[part].astype(BF16)


def attend_kernel(info_ref, col_ref, row_ref, came_ref, out_ref, d_ref, e_ref):
    row, col = iota((SPAN, SPAN), 0), iota((SPAN, SPAN), 1)
    apart = jnp.where(((row & 31) << 3) + (row >> 5) == col, 1.0, 0.0).astype(BF16)
    together = jnp.where(((col & 31) << 3) + (col >> 5) == row, 1.0, 0.0).astype(BF16)

    def split(block, carry):
        base = pl.multiple_of(block * 32, 32)
        rows = jnp.concatenate(
            [
                came_ref[pl.ds(base, 32), 8 * j : 8 * j + 8, :].astype(F32).reshape(SPAN, 128)
                for j in range(7)
            ],
            axis=1,
        ).astype(BF16)
        parted = dot(apart, rows).astype(BF16)
        for j in range(7):
            for i in range(2):
                for a in range(4):
                    at = (4 * i + a) * 32
                    d_ref[a, pl.ds(pl.multiple_of((2 * j + i) * SPAN + base, 32), 32), :] = parted[
                        at : at + 32, j * 128 : (j + 1) * 128
                    ]
        return carry

    lax.fori_loop(0, 8, split, 0)
    for b in range(4):
        e_ref[b, 12 * SPAN :, :] = jnp.zeros((2 * SPAN, 128), BF16)

    def pages_of_two(it, carry):
        start = pl.multiple_of(it * (2 * SPAN), 2 * SPAN)
        attend_unit(d_ref, e_ref, col_ref, row_ref, start, None, it // 6, 2)
        return carry

    def pages_of_three(it, carry):
        is_heavy = info_ref[5]
        start = pl.multiple_of(jnp.where(is_heavy > 0, it * (2 * SPAN), 10 * SPAN), 2 * SPAN)
        third = pl.multiple_of(jnp.where(is_heavy > 0, (8 + it) * SPAN, 12 * SPAN), SPAN)
        attend_unit(d_ref, e_ref, col_ref, row_ref, start, third, 1 - is_heavy, 3)
        return carry

    lax.fori_loop(0, info_ref[1], pages_of_two, 0)
    lax.fori_loop(0, info_ref[2], pages_of_three, 0)

    def join(block, carry):
        base = pl.multiple_of(block * 32, 32)
        rows = jnp.concatenate(
            [
                jnp.concatenate(
                    [
                        e_ref[b, pl.ds(pl.multiple_of((2 * j + i) * SPAN + base, 32), 32), :]
                        for i in range(2)
                        for b in range(4)
                    ],
                    axis=0,
                )
                for j in range(7)
            ],
            axis=1,
        )
        joined = dot(together, rows)
        for j in range(7):
            tile = joined[:, j * 128 : (j + 1) * 128].reshape(32, 8, 128)
            out_ref[pl.ds(base, 32), 8 * j : 8 * j + 8, :] = tile.astype(BF16)
        return carry

    lax.fori_loop(0, 8, join, 0)


def home_kernel(codes_ref, home_ref, back_ref, o_ref, dq_ref, dk_ref, dv_ref):
    home = home_ref[...]
    home = jnp.concatenate([home] * 4, axis=1)
    pickers = [
        jnp.where(home == codes_ref[n : n + 1, :], 1.0, 0.0).astype(BF16) for n in range(CODES)
    ]
    for head in range(6):
        total = None
        for pair, parts in PAIRS:
            for part_head, n in parts:
                if part_head == head:
                    rows = jnp.concatenate(
                        [
                            back_ref[:, x, 8 * pair : 8 * pair + 8, :].astype(F32).reshape(512, 128)
                            for x in range(4)
                        ],
                        axis=1,
                    ).astype(BF16)
                    term = dot(pickers[n], rows)
                    total = term if total is None else total + term
        for b, ref in enumerate((o_ref, dq_ref, dk_ref, dv_ref)):
            for x in range(4):
                at = (6 * x + head) * HD
                ref[:, at : at + HD] = total[
                    b * 128 : (b + 1) * 128, x * 128 : (x + 1) * 128
                ].astype(BF16)


def body(queries, keys, values, upstream, dest_group, clip_ids):
    group = lax.axis_index("dp")
    device = group * 4 + lax.axis_index("seq")
    targets = dest_group.reshape(SPAN, 128)
    clips = clip_ids.reshape(SPAN, 128)
    me = jnp.stack((device, group)).astype(jnp.int32)
    vmem = pl.BlockSpec(memory_space=pltpu.VMEM)
    smem = pl.BlockSpec(memory_space=pltpu.SMEM)
    params = pltpu.CompilerParams(vmem_limit_bytes=40 * MIB)
    shape = jax.ShapeDtypeStruct
    send, codes, home, info = pl.pallas_call(
        pack_kernel,
        out_shape=(
            shape((64, 4, 4 * PAGES, 128), BF16),
            shape((CODES, 512), F32),
            shape((512, 128), F32),
            shape((8,), jnp.int32),
        ),
        in_specs=[smem] + [vmem] * 5,
        out_specs=(vmem, vmem, vmem, smem),
        compiler_params=params,
    )(me, targets, queries, keys, values, upstream)

    def paged_path():
        came = lax.all_to_all(
            send.reshape(SPAN, 4 * PAGES, 128), ("dp", "seq"), split_axis=0, concat_axis=0, tiled=True
        )
        col, row = pl.pallas_call(
            label_kernel,
            out_shape=(shape((2, 3 * SPAN, 128), F32), shape((2, 8, 3 * SPAN), F32)),
            in_specs=[smem, vmem, vmem],
            out_specs=(vmem, vmem),
            compiler_params=params,
        )(info, targets, clips)
        out = pl.pallas_call(
            attend_kernel,
            out_shape=shape((SPAN, 4 * PAGES, 128), BF16),
            in_specs=[smem, vmem, vmem, vmem],
            out_specs=vmem,
            scratch_shapes=[
                pltpu.VMEM((4, PAGES * SPAN, 128), BF16),
                pltpu.VMEM((4, PAGES * SPAN, 128), BF16),
            ],
            compiler_params=params,
        )(info, col, row, came)
        back = lax.all_to_all(out, ("dp", "seq"), split_axis=0, concat_axis=0, tiled=True)
        return tuple(
            pl.pallas_call(
                home_kernel,
                out_shape=(shape(queries.shape, BF16),) * 4,
                in_specs=[vmem] * 3,
                out_specs=(vmem,) * 4,
                compiler_params=params,
            )(codes, home, back.reshape(64, 4, 4 * PAGES, 128))
        )

    return lax.cond(
        info[0] <= HEAVY_MAX,
        paged_path,
        lambda: plain_path(queries, keys, values, upstream, dest_group, clip_ids),
    )


def solution(mesh):
    return jax.shard_map(
        body,
        mesh=mesh,
        in_specs=(
            P(("dp", "seq"), None),
            P(("dp", "seq"), None),
            P(("dp", "seq"), None),
            P(("dp", "seq"), None),
            P(),
            P(),
        ),
        out_specs=(
            P(("dp", "seq"), None),
            P(("dp", "seq"), None),
            P(("dp", "seq"), None),
            P(("dp", "seq"), None),
        ),
        check_vma=False,
    )
```

```python
import jax
import jax.numpy as jnp
from jax import lax
from jax.experimental import pallas as pl
from jax.experimental.pallas import tpu as pltpu
from jax.sharding import PartitionSpec as P

HD = 128


def prior_count(targets):
    length = targets.shape[-1]
    earlier = lax.broadcasted_iota(jnp.int32, (length, length), 1) < lax.broadcasted_iota(
        jnp.int32, (length, length), 0
    )
    matching = targets[..., :, None] == targets[..., None, :]
    return jnp.sum((matching & earlier).astype(jnp.int32), axis=-1)


def slot_labels(targets, clip_table, group_index, capacity):
    arriving = targets == group_index
    row_ranks = prior_count(targets)
    slot_ids = lax.broadcasted_iota(jnp.int32, (capacity,), 0)
    filled = arriving[:, None, :] & (row_ranks[:, None, :] == slot_ids[None, :, None])
    return jnp.sum(jnp.where(filled, clip_table[:, None, :] + 1, 0), axis=-1)


def return_rows(positions, slot_count, stacked):
    picker = (
        positions[:, None] == lax.broadcasted_iota(jnp.int32, (positions.shape[0], slot_count), 1)
    ).astype(jnp.bfloat16)
    return jnp.einsum("ts,nsc->ntc", picker, stacked, preferred_element_type=jnp.float32).astype(
        jnp.bfloat16
    )


def attend_forward(query_rows, key_rows, value_rows, related):
    scale = HD ** (-0.5)
    contract_cols = (((1,), (1,)), ((), ()))
    prob_list, probs_b_list, out_list = ([], [], [])
    for head_index in range(query_rows.shape[1] // HD):
        lower = head_index * HD
        query_head = query_rows[:, lower : lower + HD]
        key_head = key_rows[:, lower : lower + HD]
        value_head = value_rows[:, lower : lower + HD]
        scores = (
            lax.dot_general(query_head, key_head, contract_cols, preferred_element_type=jnp.float32)
            * scale
        )
        scores = jnp.where(related, scores, -1e30)
        row_max = jnp.max(scores, axis=1, keepdims=True)
        weights = jnp.where(related, jnp.exp(scores - row_max), 0.0)
        probs = weights / jnp.sum(weights, axis=1, keepdims=True)
        probs_b = probs.astype(jnp.bfloat16)
        prob_list.append(probs)
        probs_b_list.append(probs_b)
        out_list.append(
            jnp.dot(probs_b, value_head, preferred_element_type=jnp.float32).astype(jnp.bfloat16)
        )
    return (prob_list, probs_b_list, jnp.concatenate(out_list, axis=1))


def attend_backward(
    query_rows, key_rows, value_rows, upstream_rows, attended, prob_list, probs_b_list
):
    scale = HD ** (-0.5)
    contract_cols = (((1,), (1,)), ((), ()))
    contract_rows = (((0,), (0,)), ((), ()))
    query_grads, key_grads, value_grads = ([], [], [])
    for head_index in range(query_rows.shape[1] // HD):
        lower = head_index * HD
        query_head = query_rows[:, lower : lower + HD]
        key_head = key_rows[:, lower : lower + HD]
        value_head = value_rows[:, lower : lower + HD]
        upstream_head = upstream_rows[:, lower : lower + HD]
        out_head = attended[:, lower : lower + HD]
        delta = jnp.sum(
            upstream_head.astype(jnp.float32) * out_head.astype(jnp.float32), axis=1, keepdims=True
        )
        dprobs = lax.dot_general(
            upstream_head, value_head, contract_cols, preferred_element_type=jnp.float32
        )
        dscores = (prob_list[head_index] * (dprobs - delta)).astype(jnp.bfloat16)
        query_grads.append(
            (jnp.dot(dscores, key_head, preferred_element_type=jnp.float32) * scale).astype(
                jnp.bfloat16
            )
        )
        key_grads.append(
            (
                lax.dot_general(
                    dscores, query_head, contract_rows, preferred_element_type=jnp.float32
                )
                * scale
            ).astype(jnp.bfloat16)
        )
        value_grads.append(
            lax.dot_general(
                probs_b_list[head_index],
                upstream_head,
                contract_rows,
                preferred_element_type=jnp.float32,
            ).astype(jnp.bfloat16)
        )
    return (
        jnp.concatenate(query_grads, axis=1),
        jnp.concatenate(key_grads, axis=1),
        jnp.concatenate(value_grads, axis=1),
    )


def plain_path(queries, keys, values, upstream, dest_group, clip_ids):
    group_count = lax.axis_size("dp")
    part_count = lax.axis_size("seq")
    group_index = lax.axis_index("dp")
    seq_index = lax.axis_index("seq")
    row_count = queries.shape[0]
    capacity = (3 * row_count + 2 * group_count - 1) // (2 * group_count)
    targets = dest_group[:, 0].reshape(group_count, part_count, row_count)
    clip_table = clip_ids.reshape(group_count, part_count, row_count)
    label_table = slot_labels(
        targets.reshape(group_count * part_count, row_count),
        clip_table.reshape(group_count * part_count, row_count),
        group_index,
        capacity,
    ).reshape(group_count, part_count, capacity)
    own_group = lax.dynamic_index_in_dim(targets, group_index, 0, keepdims=False)
    labels = label_table.reshape(-1)
    own_rows = lax.dynamic_index_in_dim(own_group, seq_index, 0, keepdims=False)
    positions = own_rows * capacity + prior_count(own_rows)
    slots = group_count * capacity
    picker = (
        lax.broadcasted_iota(jnp.int32, (slots, row_count), 0) == positions[None, :]
    ).astype(jnp.bfloat16)
    width = queries.shape[1] // part_count
    stacked = jnp.stack((queries, keys, values, upstream))
    packed = jnp.einsum("st,ntc->snc", picker, stacked, preferred_element_type=jnp.float32).astype(
        jnp.bfloat16
    )
    blocks = packed.reshape(group_count, capacity, 4, part_count, width)
    blocks = jnp.transpose(blocks, (0, 3, 1, 2, 4)).reshape(-1, capacity, 4, width)
    arrived = lax.all_to_all(blocks, ("dp", "seq"), split_axis=0, concat_axis=0, tiled=True)
    regrouped = jnp.transpose(arrived, (2, 0, 1, 3)).reshape(4, -1, width)
    slot_total = labels.shape[0]
    identity = lax.broadcasted_iota(jnp.int32, (slot_total, slot_total), 0) == lax.broadcasted_iota(
        jnp.int32, (slot_total, slot_total), 1
    )
    related = (labels[:, None] == labels[None, :]) & (labels[:, None] > 0) | identity
    prob_list, probs_b_list, attended = attend_forward(
        regrouped[0], regrouped[1], regrouped[2], related
    )
    gradients = attend_backward(
        regrouped[0], regrouped[1], regrouped[2], regrouped[3], attended, prob_list, probs_b_list
    )
    results = jnp.stack((attended, gradients[0], gradients[1], gradients[2]), axis=1)
    results = results.reshape(-1, capacity, 4, width)
    routed_back = lax.all_to_all(results, ("dp", "seq"), split_axis=0, concat_axis=0, tiled=True)
    routed_back = routed_back.reshape(group_count, part_count, capacity, 4, width)
    routed_back = jnp.transpose(routed_back, (3, 0, 2, 1, 4)).reshape(4, slots, -1)
    all_home = return_rows(positions, slots, routed_back)
    return (all_home[0], all_home[1], all_home[2], all_home[3])

UNITS = 6
PAGES = 13
TRADES = UNITS - 1
SPAN = 256
MIB = 1 << 20
F32 = jnp.float32
BF16 = jnp.bfloat16
ROWS_T = (((1,), (1,)), ((), ()))
COLS_T = (((0,), (0,)), ((), ()))


def iota(shape, dim):
    return lax.broadcasted_iota(jnp.int32, shape, dim)


def dot(a, b, dims=(((1,), (0,)), ((), ()))):
    return lax.dot_general(a, b, dims, preferred_element_type=F32)


def unit_table(heavy, heavy_rank):
    square = (128, 128)
    group, lane = iota(square, 0), iota(square, 1)

    def total(cond, values):
        return jnp.sum(jnp.where(cond, values, 0.0), axis=1, keepdims=True).astype(jnp.int32)

    heavy_rank = heavy_rank.astype(jnp.int32)
    lane_f = lane.astype(F32)
    is_heavy = total(lane == group, heavy) > 0
    below = total(lane < group, heavy)
    heavies = total(lane >= 0, heavy)
    rank = group[:, :1] - below
    light = (lane < 64) & (heavy < 0.5)
    trades = jnp.logical_not(is_heavy) & (rank < TRADES * heavies)
    turn = (rank * 13) >> 6
    served = total((heavy > 0.5) & (heavy_rank == turn), lane_f)
    third = jnp.where(is_heavy, 0, jnp.where(trades, rank - TRADES * turn + 1, -1))
    table = jnp.zeros(square, jnp.int32)
    for unit in range(UNITS):
        source = group[:, :1]
        if unit > 0:
            light_rank = lane - heavy_rank
            traded = total(light & (light_rank == TRADES * below + unit - 1), lane_f)
            source = jnp.where(is_heavy, traded, jnp.where(third == unit, served, source))
        table = jnp.where(lane == unit, source, table)
        table = jnp.where(lane == UNITS + unit, jnp.where(third == unit, 3 * source + 2, -1), table)
    return jnp.where(lane == 2 * UNITS, third, table), heavies


def pack_kernel(
    me_ref, targets_ref, q_ref, k_ref, v_ref, u_ref, send_ref, codes_ref, thirds_ref, home_ref, info_ref
):
    device, group = me_ref[0], me_ref[1]
    targets = targets_ref[...]
    lane = iota((SPAN, 128), 1)
    ones = jnp.ones((128, 128), BF16)
    flags = jnp.zeros((SPAN, 128), jnp.int32)
    shift = 2 * (lane & 7)
    spread = jnp.left_shift(jnp.ones((SPAN, 128), jnp.int32), 2 * (targets & 7))
    for word in range(8):
        bits = jnp.where((targets >> 3) == word, spread, 0).astype(F32).astype(BF16)
        counts = dot(bits, ones).astype(jnp.int32)
        three = jnp.right_shift(counts, shift) & jnp.right_shift(counts, shift + 1) & 1
        flags = jnp.where((lane >> 3) == word, three, flags)
    heavy = jnp.max(flags.astype(F32), axis=0, keepdims=True)
    square = (128, 128)
    row, col = iota(square, 0), iota(square, 1)
    heavy = jnp.broadcast_to(heavy, square)
    earlier = jnp.where(row < col, 1.0, 0.0).astype(BF16)
    table, heavies = unit_table(heavy, dot(heavy.astype(BF16), earlier))

    table_f = table.astype(F32)
    table_b = table_f.astype(BF16)
    table_t = table_f.T[:16].astype(BF16)
    spread_c = jnp.where(iota((512, 128), 0) >> 3 == iota((512, 128), 1), 1.0, 0.0).astype(BF16)
    spread_l = jnp.where(iota((128, 512), 1) >> 3 == iota((128, 512), 0), 1.0, 0.0).astype(BF16)
    thirds_c = jnp.where(iota((256, 128), 0) >> 2 == iota((256, 128), 1), 1.0, 0.0).astype(BF16)
    thirds_l = jnp.where(iota((128, 256), 1) >> 2 == iota((128, 256), 0), 1.0, 0.0).astype(BF16)

    def two(line):
        return (4 * ((line >> 2) & 1) + (line & 3)).astype(F32)

    def one(codes, line):
        return jnp.where(codes < 0.0, -1.0, 4.0 * codes + (line & 3).astype(F32))

    pages_c = 12.0 * dot(spread_c, table_b) + two(iota((512, 128), 0))
    pages_l = 12.0 * dot(table_t, spread_l) + two(iota((16, 512), 1))
    third_c = one(dot(thirds_c, table_b), iota((256, 128), 0))
    third_l = one(dot(table_t, thirds_l), iota((16, 256), 1))
    codes_ref[...] = pages_l[:8]
    thirds_ref[...] = third_l[UNITS : UNITS + 8]

    mine = jnp.broadcast_to(targets_ref[pl.ds(device, 1), :].astype(F32), square)
    mine_c = mine.T
    same = mine == mine_c
    prior_l = jnp.sum(jnp.where(same & (row < col), 1.0, 0.0), axis=0, keepdims=True)
    prior_c = jnp.sum(jnp.where(same & (col < row), 1.0, 0.0), axis=1, keepdims=True)
    key_l = 12.0 * mine[:1] + 4.0 * prior_l
    key_c = 12.0 * mine_c + 4.0 * prior_c
    key_l = jnp.concatenate([key_l + float(a) for a in range(4)], axis=1)
    for a in range(4):
        home_ref[a * 128 : (a + 1) * 128, :] = key_c + float(a)

    extra = None
    for unit in range(UNITS):
        columns = jnp.concatenate(
            [
                jnp.concatenate(
                    [ref[:, (6 * x + unit) * HD : (6 * x + unit + 1) * HD] for x in range(4)], axis=1
                )
                for ref in (q_ref, k_ref, v_ref, u_ref)
            ],
            axis=0,
        )
        picker = jnp.where(pages_c[:, unit : unit + 1] == key_l, 1.0, 0.0).astype(BF16)
        picked = dot(picker, columns)
        for x in range(4):
            tile = picked[:, x * 128 : (x + 1) * 128].reshape(64, 2, 4, 128)
            send_ref[:, x, 2 * unit : 2 * unit + 2, :, :] = tile.astype(BF16)
        third = third_c[:, UNITS + unit : UNITS + unit + 1]
        term = dot(jnp.where(third == key_l, 1.0, 0.0).astype(BF16), columns)
        extra = term if unit == 0 else extra + term
    for x in range(4):
        tile = extra[:, x * 128 : (x + 1) * 128].reshape(64, 4, 128)
        send_ref[:, x, 2 * UNITS, :, :] = tile.astype(BF16)

    own = jnp.sum(jnp.where(row == group, table_f, 0.0), axis=0, keepdims=True)
    for unit in range(UNITS):
        info_ref[unit] = jnp.sum(jnp.where(col[:1] == unit, own, 0.0)).astype(jnp.int32)
    info_ref[UNITS] = jnp.sum(jnp.where(col[:1] == 2 * UNITS, own, 0.0)).astype(jnp.int32)
    info_ref[UNITS + 1] = jnp.sum(heavy[:1]).astype(jnp.int32)


def label_kernel(info_ref, targets_ref, clips_ref, col_ref, row_ref):
    targets = targets_ref[...]
    clips = clips_ref[...] + 1
    row, col = iota((128, 128), 0), iota((128, 128), 1)
    earlier = jnp.where(row < col, 1.0, 0.0).astype(BF16)
    ones = jnp.ones((128, 128), BF16)
    for unit in range(UNITS):
        arriving = targets == info_ref[unit]
        rank = dot(jnp.where(arriving, 1.0, 0.0).astype(BF16), earlier).astype(jnp.int32)
        for slot in range(3):
            labels = jnp.where(arriving & (rank == slot), clips, 0).astype(F32).astype(BF16)
            col_ref[unit, slot * SPAN : (slot + 1) * SPAN, :] = dot(labels, ones)
            row_ref[unit, :, slot * SPAN : (slot + 1) * SPAN] = dot(ones[:8], labels, ROWS_T)


def attend_unit(d_ref, e_ref, col_ref, row_ref, unit, count):
    scale = HD**-0.5
    start = pl.multiple_of(unit * (2 * SPAN), 2 * SPAN)
    places = [start, start + SPAN] + ([2 * UNITS * SPAN] if count == 3 else [])

    def load(a):
        return jnp.concatenate([d_ref[a, pl.ds(place, SPAN), :] for place in places], axis=0)

    key, value = load(1), load(2)
    row_labels = row_ref[unit, 0:1, : count * SPAN]
    grad_key, grad_value = None, None
    for n, place in enumerate(places):
        query = d_ref[0, pl.ds(place, SPAN), :]
        cotangent = d_ref[3, pl.ds(place, SPAN), :]
        labels = col_ref[unit, n * SPAN : (n + 1) * SPAN, :]
        related = jnp.concatenate([labels] * (2 * count), axis=1) == row_labels
        scores = jnp.where(related, dot(query, key, ROWS_T), -1e30)
        top = jnp.max(scores, axis=1, keepdims=True)
        weights = jnp.exp2((scores - top) * (scale * 1.4426950408889634))
        probs = weights * (1.0 / jnp.sum(weights, axis=1, keepdims=True))
        probs_b = probs.astype(BF16)
        attended = dot(probs_b, value).astype(BF16)
        delta = jnp.sum(cotangent.astype(F32) * attended.astype(F32), axis=1, keepdims=True)
        dscores = (probs * (dot(cotangent, value, ROWS_T) - delta)).astype(BF16)
        e_ref[0, pl.ds(place, SPAN), :] = attended
        e_ref[1, pl.ds(place, SPAN), :] = (dot(dscores, key) * scale).astype(BF16)
        term_key = dot(dscores, query, COLS_T)
        term_value = dot(probs_b, cotangent, COLS_T)
        grad_key = term_key if n == 0 else grad_key + term_key
        grad_value = term_value if n == 0 else grad_value + term_value
    for n, place in enumerate(places):
        part = slice(n * SPAN, (n + 1) * SPAN)
        e_ref[2, pl.ds(place, SPAN), :] = (grad_key[part] * scale).astype(BF16)
        e_ref[3, pl.ds(place, SPAN), :] = grad_value[part].astype(BF16)


def attend_kernel(info_ref, col_ref, row_ref, came_ref, out_ref, d_ref, e_ref):
    row, col = iota((SPAN, SPAN), 0), iota((SPAN, SPAN), 1)
    apart = jnp.where(((row & 31) << 3) + (row >> 5) == col, 1.0, 0.0).astype(BF16)
    together = jnp.where(((col & 31) << 3) + (col >> 5) == row, 1.0, 0.0).astype(BF16)
    apart_1 = jnp.where(((row & 63) << 2) + (row >> 6) == col, 1.0, 0.0).astype(BF16)
    together_1 = jnp.where(((col & 63) << 2) + (col >> 6) == row, 1.0, 0.0).astype(BF16)
    last = 2 * UNITS

    def split(block, carry):
        base = pl.multiple_of(block * 32, 32)
        rows = jnp.concatenate(
            [
                came_ref[pl.ds(base, 32), 2 * j : 2 * j + 2, :, :].astype(F32).reshape(SPAN, 128)
                for j in range(UNITS)
            ],
            axis=1,
        ).astype(BF16)
        parted = dot(apart, rows).astype(BF16)
        for j in range(UNITS):
            for i in range(2):
                for a in range(4):
                    at = (4 * i + a) * 32
                    d_ref[a, pl.ds(pl.multiple_of((2 * j + i) * SPAN + base, 32), 32), :] = parted[
                        at : at + 32, j * 128 : (j + 1) * 128
                    ]
        return carry

    lax.fori_loop(0, 8, split, 0)
    rows = jnp.concatenate(
        [
            came_ref[n * 64 : (n + 1) * 64, last, :, :].astype(F32).reshape(SPAN, 128)
            for n in range(4)
        ],
        axis=1,
    ).astype(BF16)
    parted = dot(apart_1, rows).astype(BF16)
    for n in range(4):
        for a in range(4):
            at = last * SPAN + n * 64
            d_ref[a, at : at + 64, :] = parted[a * 64 : (a + 1) * 64, n * 128 : (n + 1) * 128]
    for b in range(4):
        e_ref[b, last * SPAN :, :] = jnp.zeros((SPAN, 128), BF16)

    third = info_ref[UNITS]

    def each_unit(unit, carry):
        @pl.when(unit == third)
        def _():
            attend_unit(d_ref, e_ref, col_ref, row_ref, unit, 3)

        @pl.when(unit != third)
        def _():
            attend_unit(d_ref, e_ref, col_ref, row_ref, unit, 2)

        return carry

    lax.fori_loop(0, UNITS, each_unit, 0)

    def join(block, carry):
        base = pl.multiple_of(block * 32, 32)
        rows = jnp.concatenate(
            [
                jnp.concatenate(
                    [
                        e_ref[b, pl.ds(pl.multiple_of((2 * j + i) * SPAN + base, 32), 32), :]
                        for i in range(2)
                        for b in range(4)
                    ],
                    axis=0,
                )
                for j in range(UNITS)
            ],
            axis=1,
        )
        joined = dot(together, rows)
        for j in range(UNITS):
            tile = joined[:, j * 128 : (j + 1) * 128].reshape(32, 2, 4, 128)
            out_ref[pl.ds(base, 32), 2 * j : 2 * j + 2, :, :] = tile.astype(BF16)
        return carry

    lax.fori_loop(0, 8, join, 0)
    rows = jnp.concatenate(
        [
            jnp.concatenate(
                [e_ref[b, last * SPAN + n * 64 : last * SPAN + (n + 1) * 64, :] for b in range(4)],
                axis=0,
            )
            for n in range(4)
        ],
        axis=1,
    )
    joined = dot(together_1, rows)
    for n in range(4):
        tile = joined[:, n * 128 : (n + 1) * 128].reshape(64, 4, 128)
        out_ref[n * 64 : (n + 1) * 64, last, :, :] = tile.astype(BF16)


def home_kernel(codes_ref, thirds_ref, home_ref, back_ref, o_ref, dq_ref, dk_ref, dv_ref):
    home = home_ref[...]
    home_2 = jnp.concatenate([home] * 2, axis=1)
    home_4 = jnp.concatenate([home] * 4, axis=1)
    extra = jnp.concatenate(
        [back_ref[:, x, 2 * UNITS, :, :].astype(F32).reshape(256, 128) for x in range(4)], axis=1
    ).astype(BF16)
    for unit in range(UNITS):
        rows = jnp.concatenate(
            [
                back_ref[:, x, 2 * unit : 2 * unit + 2, :, :].astype(F32).reshape(512, 128)
                for x in range(4)
            ],
            axis=1,
        ).astype(BF16)
        picker = jnp.where(home_4 == codes_ref[unit : unit + 1, :], 1.0, 0.0).astype(BF16)
        third = jnp.where(home_2 == thirds_ref[unit : unit + 1, :], 1.0, 0.0).astype(BF16)
        total = dot(picker, rows) + dot(third, extra)
        for b, ref in enumerate((o_ref, dq_ref, dk_ref, dv_ref)):
            for x in range(4):
                at = (6 * x + unit) * HD
                ref[:, at : at + HD] = total[
                    b * 128 : (b + 1) * 128, x * 128 : (x + 1) * 128
                ].astype(BF16)


VMEM = pl.BlockSpec(memory_space=pltpu.VMEM)
SMEM = pl.BlockSpec(memory_space=pltpu.SMEM)
SHAPE = jax.ShapeDtypeStruct


def kernel_params():
    return pltpu.CompilerParams(vmem_limit_bytes=40 * MIB)


def pack(me, targets, arrays):
    return pl.pallas_call(
        pack_kernel,
        out_shape=(
            SHAPE((64, 4, PAGES, 4, 128), BF16),
            SHAPE((8, 512), F32),
            SHAPE((8, 256), F32),
            SHAPE((512, 128), F32),
            SHAPE((8,), jnp.int32),
        ),
        in_specs=[SMEM] + [VMEM] * 5,
        out_specs=(VMEM, VMEM, VMEM, VMEM, SMEM),
        compiler_params=kernel_params(),
    )(me, targets, *arrays)


def label(info, targets, clips):
    return pl.pallas_call(
        label_kernel,
        out_shape=(SHAPE((UNITS, 3 * SPAN, 128), F32), SHAPE((UNITS, 8, 3 * SPAN), F32)),
        in_specs=[SMEM, VMEM, VMEM],
        out_specs=(VMEM, VMEM),
        compiler_params=kernel_params(),
    )(info, targets, clips)


def attend(info, col, row, came):
    return pl.pallas_call(
        attend_kernel,
        out_shape=SHAPE((SPAN, PAGES, 4, 128), BF16),
        in_specs=[SMEM, VMEM, VMEM, VMEM],
        out_specs=VMEM,
        scratch_shapes=[
            pltpu.VMEM((4, PAGES * SPAN, 128), BF16),
            pltpu.VMEM((4, PAGES * SPAN, 128), BF16),
        ],
        compiler_params=kernel_params(),
    )(info, col, row, came)


def unpack(codes, thirds, home, back):
    return pl.pallas_call(
        home_kernel,
        out_shape=(SHAPE((128, 24 * HD), BF16),) * 4,
        in_specs=[VMEM] * 4,
        out_specs=(VMEM,) * 4,
        compiler_params=kernel_params(),
    )(codes, thirds, home, back)


def body(queries, keys, values, upstream, dest_group, clip_ids):
    group = lax.axis_index("dp")
    device = group * 4 + lax.axis_index("seq")
    targets = dest_group.reshape(SPAN, 128)
    clips = clip_ids.reshape(SPAN, 128)
    me = jnp.stack((device, group)).astype(jnp.int32)
    arrays = (queries, keys, values, upstream)
    send, codes, thirds, home, info = pack(me, targets, arrays)

    def exchange(blocks):
        return lax.all_to_all(blocks, ("dp", "seq"), split_axis=0, concat_axis=0, tiled=True)

    def paged_path():
        came = exchange(send.reshape(SPAN, PAGES, 4, 128))
        col, row = label(info, targets, clips)
        back = exchange(attend(info, col, row, came))
        return tuple(unpack(codes, thirds, home, back.reshape(64, 4, PAGES, 4, 128)))

    return lax.cond(
        UNITS * info[UNITS + 1] <= 64,
        paged_path,
        lambda: plain_path(queries, keys, values, upstream, dest_group, clip_ids),
    )


def solution(mesh):
    return jax.shard_map(
        body,
        mesh=mesh,
        in_specs=(
            P(("dp", "seq"), None),
            P(("dp", "seq"), None),
            P(("dp", "seq"), None),
            P(("dp", "seq"), None),
            P(),
            P(),
        ),
        out_specs=(
            P(("dp", "seq"), None),
            P(("dp", "seq"), None),
            P(("dp", "seq"), None),
            P(("dp", "seq"), None),
        ),
        check_vma=False,
    )
```

```python
import jax
import jax.numpy as jnp
from jax import lax
from jax.experimental import pallas as pl
from jax.experimental.pallas import tpu as pltpu
from jax.sharding import PartitionSpec as P

HD = 128


def prior_count(targets):
    length = targets.shape[-1]
    earlier = lax.broadcasted_iota(jnp.int32, (length, length), 1) < lax.broadcasted_iota(
        jnp.int32, (length, length), 0
    )
    matching = targets[..., :, None] == targets[..., None, :]
    return jnp.sum((matching & earlier).astype(jnp.int32), axis=-1)


def slot_labels(targets, clip_table, group_index, capacity):
    arriving = targets == group_index
    row_ranks = prior_count(targets)
    slot_ids = lax.broadcasted_iota(jnp.int32, (capacity,), 0)
    filled = arriving[:, None, :] & (row_ranks[:, None, :] == slot_ids[None, :, None])
    return jnp.sum(jnp.where(filled, clip_table[:, None, :] + 1, 0), axis=-1)


def return_rows(positions, slot_count, stacked):
    picker = (
        positions[:, None] == lax.broadcasted_iota(jnp.int32, (positions.shape[0], slot_count), 1)
    ).astype(jnp.bfloat16)
    return jnp.einsum("ts,nsc->ntc", picker, stacked, preferred_element_type=jnp.float32).astype(
        jnp.bfloat16
    )


def attend_forward(query_rows, key_rows, value_rows, related):
    scale = HD ** (-0.5)
    contract_cols = (((1,), (1,)), ((), ()))
    prob_list, probs_b_list, out_list = ([], [], [])
    for head_index in range(query_rows.shape[1] // HD):
        lower = head_index * HD
        query_head = query_rows[:, lower : lower + HD]
        key_head = key_rows[:, lower : lower + HD]
        value_head = value_rows[:, lower : lower + HD]
        scores = (
            lax.dot_general(query_head, key_head, contract_cols, preferred_element_type=jnp.float32)
            * scale
        )
        scores = jnp.where(related, scores, -1e30)
        row_max = jnp.max(scores, axis=1, keepdims=True)
        weights = jnp.where(related, jnp.exp(scores - row_max), 0.0)
        probs = weights / jnp.sum(weights, axis=1, keepdims=True)
        probs_b = probs.astype(jnp.bfloat16)
        prob_list.append(probs)
        probs_b_list.append(probs_b)
        out_list.append(
            jnp.dot(probs_b, value_head, preferred_element_type=jnp.float32).astype(jnp.bfloat16)
        )
    return (prob_list, probs_b_list, jnp.concatenate(out_list, axis=1))


def attend_backward(
    query_rows, key_rows, value_rows, upstream_rows, attended, prob_list, probs_b_list
):
    scale = HD ** (-0.5)
    contract_cols = (((1,), (1,)), ((), ()))
    contract_rows = (((0,), (0,)), ((), ()))
    query_grads, key_grads, value_grads = ([], [], [])
    for head_index in range(query_rows.shape[1] // HD):
        lower = head_index * HD
        query_head = query_rows[:, lower : lower + HD]
        key_head = key_rows[:, lower : lower + HD]
        value_head = value_rows[:, lower : lower + HD]
        upstream_head = upstream_rows[:, lower : lower + HD]
        out_head = attended[:, lower : lower + HD]
        delta = jnp.sum(
            upstream_head.astype(jnp.float32) * out_head.astype(jnp.float32), axis=1, keepdims=True
        )
        dprobs = lax.dot_general(
            upstream_head, value_head, contract_cols, preferred_element_type=jnp.float32
        )
        dscores = (prob_list[head_index] * (dprobs - delta)).astype(jnp.bfloat16)
        query_grads.append(
            (jnp.dot(dscores, key_head, preferred_element_type=jnp.float32) * scale).astype(
                jnp.bfloat16
            )
        )
        key_grads.append(
            (
                lax.dot_general(
                    dscores, query_head, contract_rows, preferred_element_type=jnp.float32
                )
                * scale
            ).astype(jnp.bfloat16)
        )
        value_grads.append(
            lax.dot_general(
                probs_b_list[head_index],
                upstream_head,
                contract_rows,
                preferred_element_type=jnp.float32,
            ).astype(jnp.bfloat16)
        )
    return (
        jnp.concatenate(query_grads, axis=1),
        jnp.concatenate(key_grads, axis=1),
        jnp.concatenate(value_grads, axis=1),
    )


def plain_path(queries, keys, values, upstream, dest_group, clip_ids):
    group_count = lax.axis_size("dp")
    part_count = lax.axis_size("seq")
    group_index = lax.axis_index("dp")
    seq_index = lax.axis_index("seq")
    row_count = queries.shape[0]
    capacity = (3 * row_count + 2 * group_count - 1) // (2 * group_count)
    targets = dest_group[:, 0].reshape(group_count, part_count, row_count)
    clip_table = clip_ids.reshape(group_count, part_count, row_count)
    label_table = slot_labels(
        targets.reshape(group_count * part_count, row_count),
        clip_table.reshape(group_count * part_count, row_count),
        group_index,
        capacity,
    ).reshape(group_count, part_count, capacity)
    own_group = lax.dynamic_index_in_dim(targets, group_index, 0, keepdims=False)
    labels = label_table.reshape(-1)
    own_rows = lax.dynamic_index_in_dim(own_group, seq_index, 0, keepdims=False)
    positions = own_rows * capacity + prior_count(own_rows)
    slots = group_count * capacity
    picker = (
        lax.broadcasted_iota(jnp.int32, (slots, row_count), 0) == positions[None, :]
    ).astype(jnp.bfloat16)
    width = queries.shape[1] // part_count
    stacked = jnp.stack((queries, keys, values, upstream))
    packed = jnp.einsum("st,ntc->snc", picker, stacked, preferred_element_type=jnp.float32).astype(
        jnp.bfloat16
    )
    blocks = packed.reshape(group_count, capacity, 4, part_count, width)
    blocks = jnp.transpose(blocks, (0, 3, 1, 2, 4)).reshape(-1, capacity, 4, width)
    arrived = lax.all_to_all(blocks, ("dp", "seq"), split_axis=0, concat_axis=0, tiled=True)
    regrouped = jnp.transpose(arrived, (2, 0, 1, 3)).reshape(4, -1, width)
    slot_total = labels.shape[0]
    identity = lax.broadcasted_iota(jnp.int32, (slot_total, slot_total), 0) == lax.broadcasted_iota(
        jnp.int32, (slot_total, slot_total), 1
    )
    related = (labels[:, None] == labels[None, :]) & (labels[:, None] > 0) | identity
    prob_list, probs_b_list, attended = attend_forward(
        regrouped[0], regrouped[1], regrouped[2], related
    )
    gradients = attend_backward(
        regrouped[0], regrouped[1], regrouped[2], regrouped[3], attended, prob_list, probs_b_list
    )
    results = jnp.stack((attended, gradients[0], gradients[1], gradients[2]), axis=1)
    results = results.reshape(-1, capacity, 4, width)
    routed_back = lax.all_to_all(results, ("dp", "seq"), split_axis=0, concat_axis=0, tiled=True)
    routed_back = routed_back.reshape(group_count, part_count, capacity, 4, width)
    routed_back = jnp.transpose(routed_back, (3, 0, 2, 1, 4)).reshape(4, slots, -1)
    all_home = return_rows(positions, slots, routed_back)
    return (all_home[0], all_home[1], all_home[2], all_home[3])

UNITS = 6
PAGES = 13
TRADES = UNITS - 1
SPAN = 256
MIB = 1 << 20
F32 = jnp.float32
BF16 = jnp.bfloat16
ROWS_T = (((1,), (1,)), ((), ()))
COLS_T = (((0,), (0,)), ((), ()))


def iota(shape, dim):
    return lax.broadcasted_iota(jnp.int32, shape, dim)


def dot(a, b, dims=(((1,), (0,)), ((), ()))):
    return lax.dot_general(a, b, dims, preferred_element_type=F32)


def unit_table(heavy, heavy_rank):
    square = (128, 128)
    group, lane = iota(square, 0), iota(square, 1)

    def total(cond, values):
        return jnp.sum(jnp.where(cond, values, 0.0), axis=1, keepdims=True).astype(jnp.int32)

    heavy_rank = heavy_rank.astype(jnp.int32)
    lane_f = lane.astype(F32)
    is_heavy = total(lane == group, heavy) > 0
    below = total(lane < group, heavy)
    heavies = total(lane >= 0, heavy)
    rank = group[:, :1] - below
    light = (lane < 64) & (heavy < 0.5)
    trades = jnp.logical_not(is_heavy) & (rank < TRADES * heavies)
    turn = (rank * 13) >> 6
    served = total((heavy > 0.5) & (heavy_rank == turn), lane_f)
    third = jnp.where(is_heavy, 0, jnp.where(trades, rank - TRADES * turn + 1, -1))
    table = jnp.zeros(square, jnp.int32)
    for unit in range(UNITS):
        source = group[:, :1]
        if unit > 0:
            light_rank = lane - heavy_rank
            traded = total(light & (light_rank == TRADES * below + unit - 1), lane_f)
            source = jnp.where(is_heavy, traded, jnp.where(third == unit, served, source))
        table = jnp.where(lane == unit, source, table)
        table = jnp.where(lane == UNITS + unit, jnp.where(third == unit, 3 * source + 2, -1), table)
    return jnp.where(lane == 2 * UNITS, third, table), heavies


def pack_kernel(
    me_ref,
    targets_ref,
    clips_ref,
    q_ref,
    k_ref,
    v_ref,
    u_ref,
    send_ref,
    codes_ref,
    thirds_ref,
    home_ref,
    marks_ref,
    info_ref,
    heavies_ref,
):
    device, group = me_ref[0], me_ref[1]
    targets = targets_ref[...]
    marks_ref[...] = 4 * targets + clips_ref[...] + 1
    lane = iota((SPAN, 128), 1)
    ones = jnp.ones((128, 128), BF16)
    flags = jnp.zeros((SPAN, 128), jnp.int32)
    shift = 2 * (lane & 7)
    spread = jnp.left_shift(jnp.ones((SPAN, 128), jnp.int32), 2 * (targets & 7))
    for word in range(8):
        bits = jnp.where((targets >> 3) == word, spread, 0).astype(F32).astype(BF16)
        counts = dot(bits, ones).astype(jnp.int32)
        three = jnp.right_shift(counts, shift) & jnp.right_shift(counts, shift + 1) & 1
        flags = jnp.where((lane >> 3) == word, three, flags)
    heavy = jnp.max(flags.astype(F32), axis=0, keepdims=True)
    square = (128, 128)
    row, col = iota(square, 0), iota(square, 1)
    heavy = jnp.broadcast_to(heavy, square)
    earlier = jnp.where(row < col, 1.0, 0.0).astype(BF16)
    table, heavies = unit_table(heavy, dot(heavy.astype(BF16), earlier))

    table_f = table.astype(F32)
    table_b = table_f.astype(BF16)
    table_t = table_f.T[:16].astype(BF16)
    spread_c = jnp.where(iota((512, 128), 0) >> 3 == iota((512, 128), 1), 1.0, 0.0).astype(BF16)
    spread_l = jnp.where(iota((128, 512), 1) >> 3 == iota((128, 512), 0), 1.0, 0.0).astype(BF16)
    thirds_c = jnp.where(iota((256, 128), 0) >> 2 == iota((256, 128), 1), 1.0, 0.0).astype(BF16)
    thirds_l = jnp.where(iota((128, 256), 1) >> 2 == iota((128, 256), 0), 1.0, 0.0).astype(BF16)

    def two(line):
        return (4 * ((line >> 2) & 1) + (line & 3)).astype(F32)

    def one(codes, line):
        return jnp.where(codes < 0.0, -1.0, 4.0 * codes + (line & 3).astype(F32))

    pages_c = 12.0 * dot(spread_c, table_b) + two(iota((512, 128), 0))
    pages_l = 12.0 * dot(table_t, spread_l) + two(iota((16, 512), 1))
    third_c = one(dot(thirds_c, table_b), iota((256, 128), 0))
    third_l = one(dot(table_t, thirds_l), iota((16, 256), 1))
    codes_ref[...] = pages_l[:8]
    thirds_ref[...] = third_l[UNITS : UNITS + 8]

    mine = jnp.broadcast_to(targets_ref[pl.ds(device, 1), :].astype(F32), square)
    mine_c = mine.T
    same = mine == mine_c
    prior_l = jnp.sum(jnp.where(same & (row < col), 1.0, 0.0), axis=0, keepdims=True)
    prior_c = jnp.sum(jnp.where(same & (col < row), 1.0, 0.0), axis=1, keepdims=True)
    key_l = 12.0 * mine[:1] + 4.0 * prior_l
    key_c = 12.0 * mine_c + 4.0 * prior_c
    key_l = jnp.concatenate([key_l + float(a) for a in range(4)], axis=1)
    for a in range(4):
        home_ref[a * 128 : (a + 1) * 128, :] = key_c + float(a)

    extra = None
    for unit in range(UNITS):
        columns = jnp.concatenate(
            [
                jnp.concatenate(
                    [ref[:, (6 * x + unit) * HD : (6 * x + unit + 1) * HD] for x in range(4)], axis=1
                )
                for ref in (q_ref, k_ref, v_ref, u_ref)
            ],
            axis=0,
        )
        picker = jnp.where(pages_c[:, unit : unit + 1] == key_l, 1.0, 0.0).astype(BF16)
        picked = dot(picker, columns)
        for x in range(4):
            tile = picked[:, x * 128 : (x + 1) * 128].reshape(64, 2, 4, 128)
            send_ref[:, x, 2 * unit : 2 * unit + 2, :, :] = tile.astype(BF16)
        third = third_c[:, UNITS + unit : UNITS + unit + 1]
        term = dot(jnp.where(third == key_l, 1.0, 0.0).astype(BF16), columns)
        extra = term if unit == 0 else extra + term
    for x in range(4):
        tile = extra[:, x * 128 : (x + 1) * 128].reshape(64, 4, 128)
        send_ref[:, x, 2 * UNITS, :, :] = tile.astype(BF16)

    own = jnp.sum(jnp.where(row == group, table_f, 0.0), axis=0, keepdims=True)
    for unit in range(UNITS):
        info_ref[unit] = jnp.sum(jnp.where(col[:1] == unit, own, 0.0)).astype(jnp.int32)
    info_ref[UNITS] = jnp.sum(jnp.where(col[:1] == 2 * UNITS, own, 0.0)).astype(jnp.int32)
    heavies_ref[0] = jnp.sum(heavy[:1]).astype(jnp.int32)


def label_kernel(info_ref, marks_ref, row_ref):
    targets = marks_ref[...] >> 2
    clips = marks_ref[...] & 3
    row, col = iota((128, 128), 0), iota((128, 128), 1)
    earlier = jnp.where(row < col, 1.0, 0.0).astype(BF16)
    ones = jnp.ones((128, 128), BF16)
    for unit in range(UNITS):
        arriving = targets == info_ref[unit]
        rank = dot(jnp.where(arriving, 1.0, 0.0).astype(BF16), earlier).astype(jnp.int32)
        for slot in range(3):
            labels = jnp.where(arriving & (rank == slot), clips, 0).astype(F32).astype(BF16)
            row_ref[unit, :, slot * SPAN : (slot + 1) * SPAN] = dot(ones[:8], labels, ROWS_T)


def attend_units(d_ref, e_ref, row_ref, units):
    scale = HD**-0.5
    everything = []
    for unit, count in units:
        start = pl.multiple_of(unit * (2 * SPAN), 2 * SPAN)
        spans = [(start, 2 * SPAN)] + ([(2 * UNITS * SPAN, SPAN)] if count == 3 else [])

        def load(a, spans=spans):
            parts = [d_ref[a, pl.ds(place, size), :] for place, size in spans]
            return parts[0] if len(parts) == 1 else jnp.concatenate(parts, axis=0)

        labels = row_ref[unit, :, : count * SPAN]
        first = jnp.where(iota((8, 128), 0) == 0, 1.0, 0.0).astype(BF16)
        column = dot(labels.astype(BF16), first, COLS_T)
        related = jnp.concatenate([column] * (2 * count), axis=1) == labels[:1]
        query, key, value, cotangent = load(0), load(1), load(2), load(3)
        scores = dot(query, key, ROWS_T)
        dprobs = dot(cotangent, value, ROWS_T)
        everything.append([spans, query, key, value, cotangent, related, scores, dprobs])
    for state in everything:
        related, scores = state[5], state[6]
        scores = jnp.where(related, scores, -1e30)
        top = jnp.max(scores, axis=1, keepdims=True)
        weights = jnp.exp2((scores - top) * (scale * 1.4426950408889634))
        probs = weights * (1.0 / jnp.sum(weights, axis=1, keepdims=True))
        state += [probs, probs.astype(BF16)]
    for spans, query, key, value, cotangent, related, scores, dprobs, probs, probs_b in everything:
        attended = dot(probs_b, value).astype(BF16)
        delta = jnp.sum(cotangent.astype(F32) * attended.astype(F32), axis=1, keepdims=True)
        dscores = (probs * (dprobs - delta)).astype(BF16)
        results = (
            attended,
            (dot(dscores, key) * scale).astype(BF16),
            (dot(query, dscores, COLS_T) * scale).T.astype(BF16),
            dot(cotangent, probs_b, COLS_T).T.astype(BF16),
        )
        for b, result in enumerate(results):
            at = 0
            for place, size in spans:
                e_ref[b, pl.ds(place, size), :] = result[at : at + size]
                at += size


def attend_kernel(info_ref, row_ref, came_ref, out_ref, d_ref, e_ref):
    row, col = iota((SPAN, SPAN), 0), iota((SPAN, SPAN), 1)
    apart = jnp.where(((row & 31) << 3) + (row >> 5) == col, 1.0, 0.0).astype(BF16)
    together = jnp.where(((col & 31) << 3) + (col >> 5) == row, 1.0, 0.0).astype(BF16)
    apart_1 = jnp.where(((row & 63) << 2) + (row >> 6) == col, 1.0, 0.0).astype(BF16)
    together_1 = jnp.where(((col & 63) << 2) + (col >> 6) == row, 1.0, 0.0).astype(BF16)
    last = 2 * UNITS

    def split(block, carry):
        base = pl.multiple_of(block * 32, 32)
        rows = jnp.concatenate(
            [
                came_ref[pl.ds(base, 32), 2 * j : 2 * j + 2, :, :].astype(F32).reshape(SPAN, 128)
                for j in range(UNITS)
            ],
            axis=1,
        ).astype(BF16)
        parted = dot(apart, rows).astype(BF16)
        for j in range(UNITS):
            for i in range(2):
                for a in range(4):
                    at = (4 * i + a) * 32
                    d_ref[a, pl.ds(pl.multiple_of((2 * j + i) * SPAN + base, 32), 32), :] = parted[
                        at : at + 32, j * 128 : (j + 1) * 128
                    ]
        return carry

    lax.fori_loop(0, 8, split, 0, unroll=8)
    rows = jnp.concatenate(
        [
            came_ref[n * 64 : (n + 1) * 64, last, :, :].astype(F32).reshape(SPAN, 128)
            for n in range(4)
        ],
        axis=1,
    ).astype(BF16)
    parted = dot(apart_1, rows).astype(BF16)
    for n in range(4):
        for a in range(4):
            at = last * SPAN + n * 64
            d_ref[a, at : at + 64, :] = parted[a * 64 : (a + 1) * 64, n * 128 : (n + 1) * 128]
    for b in range(4):
        e_ref[b, last * SPAN :, :] = jnp.zeros((SPAN, 128), BF16)

    third = info_ref[UNITS]

    def each_pair(pair, carry):
        @pl.when(pair == third >> 1)
        def _():
            attend_units(d_ref, e_ref, row_ref, ((third, 3), (third ^ 1, 2)))

        @pl.when(pair != third >> 1)
        def _():
            attend_units(d_ref, e_ref, row_ref, ((2 * pair, 2), (2 * pair + 1, 2)))

        return carry

    lax.fori_loop(0, UNITS // 2, each_pair, 0)

    def join(block, carry):
        base = pl.multiple_of(block * 32, 32)
        rows = jnp.concatenate(
            [
                jnp.concatenate(
                    [
                        e_ref[b, pl.ds(pl.multiple_of((2 * j + i) * SPAN + base, 32), 32), :]
                        for i in range(2)
                        for b in range(4)
                    ],
                    axis=0,
                )
                for j in range(UNITS)
            ],
            axis=1,
        )
        joined = dot(together, rows)
        for j in range(UNITS):
            tile = joined[:, j * 128 : (j + 1) * 128].reshape(32, 2, 4, 128)
            out_ref[pl.ds(base, 32), 2 * j : 2 * j + 2, :, :] = tile.astype(BF16)
        return carry

    lax.fori_loop(0, 8, join, 0, unroll=8)
    rows = jnp.concatenate(
        [
            jnp.concatenate(
                [e_ref[b, last * SPAN + n * 64 : last * SPAN + (n + 1) * 64, :] for b in range(4)],
                axis=0,
            )
            for n in range(4)
        ],
        axis=1,
    )
    joined = dot(together_1, rows)
    for n in range(4):
        tile = joined[:, n * 128 : (n + 1) * 128].reshape(64, 4, 128)
        out_ref[n * 64 : (n + 1) * 64, last, :, :] = tile.astype(BF16)


def home_kernel(codes_ref, thirds_ref, home_ref, back_ref, o_ref, dq_ref, dk_ref, dv_ref):
    home = home_ref[...]
    home_2 = jnp.concatenate([home] * 2, axis=1)
    home_4 = jnp.concatenate([home] * 4, axis=1)
    extra = jnp.concatenate(
        [back_ref[:, x, 2 * UNITS, :, :].astype(F32).reshape(256, 128) for x in range(4)], axis=1
    ).astype(BF16)
    for unit in range(UNITS):
        rows = jnp.concatenate(
            [
                back_ref[:, x, 2 * unit : 2 * unit + 2, :, :].astype(F32).reshape(512, 128)
                for x in range(4)
            ],
            axis=1,
        ).astype(BF16)
        picker = jnp.where(home_4 == codes_ref[unit : unit + 1, :], 1.0, 0.0).astype(BF16)
        third = jnp.where(home_2 == thirds_ref[unit : unit + 1, :], 1.0, 0.0).astype(BF16)
        total = dot(picker, rows) + dot(third, extra)
        for b, ref in enumerate((o_ref, dq_ref, dk_ref, dv_ref)):
            for x in range(4):
                at = (6 * x + unit) * HD
                ref[:, at : at + HD] = total[
                    b * 128 : (b + 1) * 128, x * 128 : (x + 1) * 128
                ].astype(BF16)


VMEM = pl.BlockSpec(memory_space=pltpu.VMEM)
SMEM = pl.BlockSpec(memory_space=pltpu.SMEM)
SHAPE = jax.ShapeDtypeStruct


def kernel_params():
    return pltpu.CompilerParams(vmem_limit_bytes=40 * MIB)


def pack(me, targets, clips, arrays):
    return pl.pallas_call(
        pack_kernel,
        out_shape=(
            SHAPE((64, 4, PAGES, 4, 128), BF16),
            SHAPE((8, 512), F32),
            SHAPE((8, 256), F32),
            SHAPE((512, 128), F32),
            SHAPE((SPAN, 128), jnp.int32),
            SHAPE((8,), jnp.int32),
            SHAPE((1,), jnp.int32),
        ),
        in_specs=[SMEM] + [VMEM] * 6,
        out_specs=(VMEM,) * 5 + (SMEM, SMEM),
        compiler_params=kernel_params(),
    )(me, targets, clips, *arrays)


def label(info, marks):
    return pl.pallas_call(
        label_kernel,
        out_shape=SHAPE((UNITS, 8, 3 * SPAN), F32),
        in_specs=[SMEM, VMEM],
        out_specs=VMEM,
        compiler_params=kernel_params(),
    )(info, marks)


def attend(info, row, came):
    return pl.pallas_call(
        attend_kernel,
        out_shape=SHAPE((SPAN, PAGES, 4, 128), BF16),
        in_specs=[SMEM, VMEM, VMEM],
        out_specs=VMEM,
        scratch_shapes=[
            pltpu.VMEM((4, PAGES * SPAN, 128), BF16),
            pltpu.VMEM((4, PAGES * SPAN, 128), BF16),
        ],
        compiler_params=kernel_params(),
    )(info, row, came)


def unpack(codes, thirds, home, back):
    return pl.pallas_call(
        home_kernel,
        out_shape=(SHAPE((128, 24 * HD), BF16),) * 4,
        in_specs=[VMEM] * 4,
        out_specs=(VMEM,) * 4,
        compiler_params=kernel_params(),
    )(codes, thirds, home, back)


def body(queries, keys, values, upstream, dest_group, clip_ids):
    group = lax.axis_index("dp")
    device = group * 4 + lax.axis_index("seq")
    targets = dest_group.reshape(SPAN, 128)
    clips = clip_ids.reshape(SPAN, 128)
    me = jnp.stack((device, group)).astype(jnp.int32)
    arrays = (queries, keys, values, upstream)
    send, codes, thirds, home, marks, info, heavies = pack(me, targets, clips, arrays)

    def exchange(blocks):
        return lax.all_to_all(blocks, ("dp", "seq"), split_axis=0, concat_axis=0, tiled=True)

    def paged_path():
        came = exchange(send.reshape(SPAN, PAGES, 4, 128))
        back = exchange(attend(info, label(info, marks), came))
        return tuple(unpack(codes, thirds, home, back.reshape(64, 4, PAGES, 4, 128)))

    return lax.cond(
        UNITS * heavies.reshape(()) <= 64,
        paged_path,
        lambda: plain_path(queries, keys, values, upstream, dest_group, clip_ids),
    )


def solution(mesh):
    return jax.shard_map(
        body,
        mesh=mesh,
        in_specs=(
            P(("dp", "seq"), None),
            P(("dp", "seq"), None),
            P(("dp", "seq"), None),
            P(("dp", "seq"), None),
            P(),
            P(),
        ),
        out_specs=(
            P(("dp", "seq"), None),
            P(("dp", "seq"), None),
            P(("dp", "seq"), None),
            P(("dp", "seq"), None),
        ),
        check_vma=False,
    )
```

```python
import jax
import jax.numpy as jnp
from jax import lax
from jax.experimental import pallas as pl
from jax.experimental.pallas import tpu as pltpu
from jax.sharding import PartitionSpec as P

HD = 128


def prior_count(targets):
    length = targets.shape[-1]
    earlier = lax.broadcasted_iota(jnp.int32, (length, length), 1) < lax.broadcasted_iota(
        jnp.int32, (length, length), 0
    )
    matching = targets[..., :, None] == targets[..., None, :]
    return jnp.sum((matching & earlier).astype(jnp.int32), axis=-1)


def slot_labels(targets, clip_table, group_index, capacity):
    arriving = targets == group_index
    row_ranks = prior_count(targets)
    slot_ids = lax.broadcasted_iota(jnp.int32, (capacity,), 0)
    filled = arriving[:, None, :] & (row_ranks[:, None, :] == slot_ids[None, :, None])
    return jnp.sum(jnp.where(filled, clip_table[:, None, :] + 1, 0), axis=-1)


def return_rows(positions, slot_count, stacked):
    picker = (
        positions[:, None] == lax.broadcasted_iota(jnp.int32, (positions.shape[0], slot_count), 1)
    ).astype(jnp.bfloat16)
    return jnp.einsum("ts,nsc->ntc", picker, stacked, preferred_element_type=jnp.float32).astype(
        jnp.bfloat16
    )


def attend_forward(query_rows, key_rows, value_rows, related):
    scale = HD ** (-0.5)
    contract_cols = (((1,), (1,)), ((), ()))
    prob_list, probs_b_list, out_list = ([], [], [])
    for head_index in range(query_rows.shape[1] // HD):
        lower = head_index * HD
        query_head = query_rows[:, lower : lower + HD]
        key_head = key_rows[:, lower : lower + HD]
        value_head = value_rows[:, lower : lower + HD]
        scores = (
            lax.dot_general(query_head, key_head, contract_cols, preferred_element_type=jnp.float32)
            * scale
        )
        scores = jnp.where(related, scores, -1e30)
        row_max = jnp.max(scores, axis=1, keepdims=True)
        weights = jnp.where(related, jnp.exp(scores - row_max), 0.0)
        probs = weights / jnp.sum(weights, axis=1, keepdims=True)
        probs_b = probs.astype(jnp.bfloat16)
        prob_list.append(probs)
        probs_b_list.append(probs_b)
        out_list.append(
            jnp.dot(probs_b, value_head, preferred_element_type=jnp.float32).astype(jnp.bfloat16)
        )
    return (prob_list, probs_b_list, jnp.concatenate(out_list, axis=1))


def attend_backward(
    query_rows, key_rows, value_rows, upstream_rows, attended, prob_list, probs_b_list
):
    scale = HD ** (-0.5)
    contract_cols = (((1,), (1,)), ((), ()))
    contract_rows = (((0,), (0,)), ((), ()))
    query_grads, key_grads, value_grads = ([], [], [])
    for head_index in range(query_rows.shape[1] // HD):
        lower = head_index * HD
        query_head = query_rows[:, lower : lower + HD]
        key_head = key_rows[:, lower : lower + HD]
        value_head = value_rows[:, lower : lower + HD]
        upstream_head = upstream_rows[:, lower : lower + HD]
        out_head = attended[:, lower : lower + HD]
        delta = jnp.sum(
            upstream_head.astype(jnp.float32) * out_head.astype(jnp.float32), axis=1, keepdims=True
        )
        dprobs = lax.dot_general(
            upstream_head, value_head, contract_cols, preferred_element_type=jnp.float32
        )
        dscores = (prob_list[head_index] * (dprobs - delta)).astype(jnp.bfloat16)
        query_grads.append(
            (jnp.dot(dscores, key_head, preferred_element_type=jnp.float32) * scale).astype(
                jnp.bfloat16
            )
        )
        key_grads.append(
            (
                lax.dot_general(
                    dscores, query_head, contract_rows, preferred_element_type=jnp.float32
                )
                * scale
            ).astype(jnp.bfloat16)
        )
        value_grads.append(
            lax.dot_general(
                probs_b_list[head_index],
                upstream_head,
                contract_rows,
                preferred_element_type=jnp.float32,
            ).astype(jnp.bfloat16)
        )
    return (
        jnp.concatenate(query_grads, axis=1),
        jnp.concatenate(key_grads, axis=1),
        jnp.concatenate(value_grads, axis=1),
    )


def plain_path(queries, keys, values, upstream, dest_group, clip_ids):
    group_count = lax.axis_size("dp")
    part_count = lax.axis_size("seq")
    group_index = lax.axis_index("dp")
    seq_index = lax.axis_index("seq")
    row_count = queries.shape[0]
    capacity = (3 * row_count + 2 * group_count - 1) // (2 * group_count)
    targets = dest_group[:, 0].reshape(group_count, part_count, row_count)
    clip_table = clip_ids.reshape(group_count, part_count, row_count)
    label_table = slot_labels(
        targets.reshape(group_count * part_count, row_count),
        clip_table.reshape(group_count * part_count, row_count),
        group_index,
        capacity,
    ).reshape(group_count, part_count, capacity)
    own_group = lax.dynamic_index_in_dim(targets, group_index, 0, keepdims=False)
    labels = label_table.reshape(-1)
    own_rows = lax.dynamic_index_in_dim(own_group, seq_index, 0, keepdims=False)
    positions = own_rows * capacity + prior_count(own_rows)
    slots = group_count * capacity
    picker = (
        lax.broadcasted_iota(jnp.int32, (slots, row_count), 0) == positions[None, :]
    ).astype(jnp.bfloat16)
    width = queries.shape[1] // part_count
    stacked = jnp.stack((queries, keys, values, upstream))
    packed = jnp.einsum("st,ntc->snc", picker, stacked, preferred_element_type=jnp.float32).astype(
        jnp.bfloat16
    )
    blocks = packed.reshape(group_count, capacity, 4, part_count, width)
    blocks = jnp.transpose(blocks, (0, 3, 1, 2, 4)).reshape(-1, capacity, 4, width)
    arrived = lax.all_to_all(blocks, ("dp", "seq"), split_axis=0, concat_axis=0, tiled=True)
    regrouped = jnp.transpose(arrived, (2, 0, 1, 3)).reshape(4, -1, width)
    slot_total = labels.shape[0]
    identity = lax.broadcasted_iota(jnp.int32, (slot_total, slot_total), 0) == lax.broadcasted_iota(
        jnp.int32, (slot_total, slot_total), 1
    )
    related = (labels[:, None] == labels[None, :]) & (labels[:, None] > 0) | identity
    prob_list, probs_b_list, attended = attend_forward(
        regrouped[0], regrouped[1], regrouped[2], related
    )
    gradients = attend_backward(
        regrouped[0], regrouped[1], regrouped[2], regrouped[3], attended, prob_list, probs_b_list
    )
    results = jnp.stack((attended, gradients[0], gradients[1], gradients[2]), axis=1)
    results = results.reshape(-1, capacity, 4, width)
    routed_back = lax.all_to_all(results, ("dp", "seq"), split_axis=0, concat_axis=0, tiled=True)
    routed_back = routed_back.reshape(group_count, part_count, capacity, 4, width)
    routed_back = jnp.transpose(routed_back, (3, 0, 2, 1, 4)).reshape(4, slots, -1)
    all_home = return_rows(positions, slots, routed_back)
    return (all_home[0], all_home[1], all_home[2], all_home[3])

UNITS = 6
PAGES = 13
TRADES = UNITS - 1
SPAN = 256
MIB = 1 << 20
F32 = jnp.float32
BF16 = jnp.bfloat16
ROWS_T = (((1,), (1,)), ((), ()))
COLS_T = (((0,), (0,)), ((), ()))


def iota(shape, dim):
    return lax.broadcasted_iota(jnp.int32, shape, dim)


def dot(a, b, dims=(((1,), (0,)), ((), ()))):
    return lax.dot_general(a, b, dims, preferred_element_type=F32)


def unit_table(heavy, heavy_rank):
    square = (128, 128)
    group, lane = iota(square, 0), iota(square, 1)

    def total(cond, values):
        return jnp.sum(jnp.where(cond, values, 0.0), axis=1, keepdims=True).astype(jnp.int32)

    heavy_rank = heavy_rank.astype(jnp.int32)
    lane_f = lane.astype(F32)
    is_heavy = total(lane == group, heavy) > 0
    below = total(lane < group, heavy)
    heavies = total(lane >= 0, heavy)
    rank = group[:, :1] - below
    light = (lane < 64) & (heavy < 0.5)
    trades = jnp.logical_not(is_heavy) & (rank < TRADES * heavies)
    turn = (rank * 13) >> 6
    served = total((heavy > 0.5) & (heavy_rank == turn), lane_f)
    third = jnp.where(is_heavy, 0, jnp.where(trades, rank - TRADES * turn + 1, -1))
    table = jnp.zeros(square, jnp.int32)
    for unit in range(UNITS):
        source = group[:, :1]
        if unit > 0:
            light_rank = lane - heavy_rank
            traded = total(light & (light_rank == TRADES * below + unit - 1), lane_f)
            source = jnp.where(is_heavy, traded, jnp.where(third == unit, served, source))
        table = jnp.where(lane == unit, source, table)
        table = jnp.where(lane == UNITS + unit, jnp.where(third == unit, 3 * source + 2, -1), table)
    return jnp.where(lane == 2 * UNITS, third, table), heavies


def pack_kernel(
    me_ref,
    targets_ref,
    clips_ref,
    q_ref,
    k_ref,
    v_ref,
    u_ref,
    send_ref,
    codes_ref,
    home_ref,
    marks_ref,
    info_ref,
    heavies_ref,
    rows_ref,
):
    device, group = me_ref[0], me_ref[1]
    targets = targets_ref[...]
    marks_ref[...] = 4 * targets + clips_ref[...] + 1
    lane = iota((SPAN, 128), 1)
    ones = jnp.ones((128, 128), BF16)
    flags = jnp.zeros((SPAN, 128), jnp.int32)
    shift = 2 * (lane & 7)
    spread = jnp.left_shift(jnp.ones((SPAN, 128), jnp.int32), 2 * (targets & 7))
    for word in range(8):
        bits = jnp.where((targets >> 3) == word, spread, 0).astype(F32).astype(BF16)
        counts = dot(bits, ones).astype(jnp.int32)
        three = jnp.right_shift(counts, shift) & jnp.right_shift(counts, shift + 1) & 1
        flags = jnp.where((lane >> 3) == word, three, flags)
    heavy = jnp.max(flags.astype(F32), axis=0, keepdims=True)
    square = (128, 128)
    row, col = iota(square, 0), iota(square, 1)
    heavy = jnp.broadcast_to(heavy, square)
    earlier = jnp.where(row < col, 1.0, 0.0).astype(BF16)
    table, heavies = unit_table(heavy, dot(heavy.astype(BF16), earlier))

    table_f = table.astype(F32)
    table_t = table_f.T
    twice_c = jnp.where(row >> 1 == col, 1.0, 0.0).astype(BF16)
    twice_l = jnp.where(col >> 1 == row, 1.0, 0.0).astype(BF16)
    pages_c = 3.0 * dot(twice_c, table_f.astype(BF16)) + (row & 1).astype(F32)
    pages_l = 3.0 * dot(table_t[:8].astype(BF16), twice_l) + (col[:8] & 1).astype(F32)
    codes_ref[:, :128] = pages_l
    codes_ref[:, 128:] = table_t[UNITS : UNITS + 8]

    mine = jnp.broadcast_to(targets_ref[pl.ds(device, 1), :].astype(F32), square)
    mine_c = mine.T
    same = mine == mine_c
    prior_l = jnp.sum(jnp.where(same & (row < col), 1.0, 0.0), axis=0, keepdims=True)
    prior_c = jnp.sum(jnp.where(same & (col < row), 1.0, 0.0), axis=1, keepdims=True)
    key_l = 3.0 * mine[:1] + prior_l
    home_ref[...] = 3.0 * mine_c + prior_c

    extra = [None] * 4
    for unit in range(UNITS):
        wanted = jnp.concatenate(
            [pages_c[:, unit : unit + 1], table_f[:64, UNITS + unit : UNITS + unit + 1]], axis=0
        )
        picker = jnp.where(wanted == key_l, 1.0, 0.0).astype(BF16)
        for a, ref in enumerate((q_ref, k_ref, v_ref, u_ref)):
            columns = jnp.concatenate(
                [ref[:, (6 * x + unit) * HD : (6 * x + unit + 1) * HD] for x in range(4)], axis=1
            )
            picked = dot(picker, columns)
            extra[a] = picked[128:] if unit == 0 else extra[a] + picked[128:]
            for x in range(4):
                rows_ref[unit % 2, x, pl.ds(a, 128, stride=4), :] = picked[
                    :128, x * 128 : (x + 1) * 128
                ]
        for x in range(4):
            tile = rows_ref[unit % 2, x].reshape(64, 2, 4, 128)
            send_ref[:, x, 2 * unit : 2 * unit + 2, :, :] = tile.astype(BF16)
    for x in range(4):
        for a in range(4):
            rows_ref[0, x, pl.ds(a, 64, stride=4), :] = extra[a][:, x * 128 : (x + 1) * 128]
        tile = rows_ref[0, x, :256, :].reshape(64, 4, 128)
        send_ref[:, x, 2 * UNITS, :, :] = tile.astype(BF16)

    own = jnp.sum(jnp.where(row == group, table_f, 0.0), axis=0, keepdims=True)
    for unit in range(UNITS):
        info_ref[unit] = jnp.sum(jnp.where(col[:1] == unit, own, 0.0)).astype(jnp.int32)
    info_ref[UNITS] = jnp.sum(jnp.where(col[:1] == 2 * UNITS, own, 0.0)).astype(jnp.int32)
    heavies_ref[0] = jnp.sum(heavy[:1]).astype(jnp.int32)


def label_kernel(info_ref, marks_ref, row_ref):
    targets = marks_ref[...] >> 2
    clips = marks_ref[...] & 3
    row, col = iota((128, 128), 0), iota((128, 128), 1)
    earlier = jnp.where(row < col, 1.0, 0.0).astype(BF16)
    ones = jnp.ones((128, 128), BF16)
    for unit in range(UNITS):
        arriving = targets == info_ref[unit]
        rank = dot(jnp.where(arriving, 1.0, 0.0).astype(BF16), earlier).astype(jnp.int32)
        for slot in range(3):
            labels = jnp.where(arriving & (rank == slot), clips, 0).astype(F32).astype(BF16)
            row_ref[unit, :, slot * SPAN : (slot + 1) * SPAN] = dot(ones[:8], labels, ROWS_T)


def attend_units(d_ref, e_ref, row_ref, units):
    scale = HD**-0.5
    everything = []
    for unit, count in units:
        start = pl.multiple_of(unit * (2 * SPAN), 2 * SPAN)
        spans = [(start, 2 * SPAN)] + ([(2 * UNITS * SPAN, SPAN)] if count == 3 else [])

        def load(a, spans=spans):
            parts = [d_ref[a, pl.ds(place, size), :] for place, size in spans]
            return parts[0] if len(parts) == 1 else jnp.concatenate(parts, axis=0)

        labels = row_ref[unit, :, : count * SPAN]
        first = jnp.where(iota((8, 128), 0) == 0, 1.0, 0.0).astype(BF16)
        column = dot(labels.astype(BF16), first, COLS_T)
        related = jnp.concatenate([column] * (2 * count), axis=1) == labels[:1]
        query, key, value, cotangent = load(0), load(1), load(2), load(3)
        scores = dot(query, key, ROWS_T)
        dprobs = dot(cotangent, value, ROWS_T)
        everything.append([spans, query, key, value, cotangent, related, scores, dprobs])
    for state in everything:
        related, scores = state[5], state[6]
        scores = jnp.where(related, scores, -1e30)
        top = jnp.max(scores, axis=1, keepdims=True)
        weights = jnp.exp2((scores - top) * (scale * 1.4426950408889634))
        probs = weights * (1.0 / jnp.sum(weights, axis=1, keepdims=True))
        state += [probs, probs.astype(BF16)]
    for spans, query, key, value, cotangent, related, scores, dprobs, probs, probs_b in everything:
        attended = dot(probs_b, value).astype(BF16)
        delta = jnp.sum(cotangent.astype(F32) * attended.astype(F32), axis=1, keepdims=True)
        dscores = (probs * (dprobs - delta)).astype(BF16)
        results = (
            attended,
            (dot(dscores, key) * scale).astype(BF16),
            (dot(query, dscores, COLS_T) * scale).T.astype(BF16),
            dot(cotangent, probs_b, COLS_T).T.astype(BF16),
        )
        for b, result in enumerate(results):
            at = 0
            for place, size in spans:
                e_ref[b, pl.ds(place, size), :] = result[at : at + size]
                at += size


def attend_kernel(info_ref, row_ref, came_ref, out_ref, d_ref, e_ref):
    row, col = iota((SPAN, SPAN), 0), iota((SPAN, SPAN), 1)
    apart = jnp.where(((row & 31) << 3) + (row >> 5) == col, 1.0, 0.0).astype(BF16)
    together = jnp.where(((col & 31) << 3) + (col >> 5) == row, 1.0, 0.0).astype(BF16)
    apart_1 = jnp.where(((row & 63) << 2) + (row >> 6) == col, 1.0, 0.0).astype(BF16)
    together_1 = jnp.where(((col & 63) << 2) + (col >> 6) == row, 1.0, 0.0).astype(BF16)
    last = 2 * UNITS

    def split(block, carry):
        base = pl.multiple_of(block * 32, 32)
        rows = jnp.concatenate(
            [
                came_ref[pl.ds(base, 32), 2 * j : 2 * j + 2, :, :].astype(F32).reshape(SPAN, 128)
                for j in range(UNITS)
            ],
            axis=1,
        ).astype(BF16)
        parted = dot(apart, rows).astype(BF16)
        for j in range(UNITS):
            for i in range(2):
                for a in range(4):
                    at = (4 * i + a) * 32
                    d_ref[a, pl.ds(pl.multiple_of((2 * j + i) * SPAN + base, 32), 32), :] = parted[
                        at : at + 32, j * 128 : (j + 1) * 128
                    ]
        return carry

    lax.fori_loop(0, 8, split, 0, unroll=8)
    rows = jnp.concatenate(
        [
            came_ref[n * 64 : (n + 1) * 64, last, :, :].astype(F32).reshape(SPAN, 128)
            for n in range(4)
        ],
        axis=1,
    ).astype(BF16)
    parted = dot(apart_1, rows).astype(BF16)
    for n in range(4):
        for a in range(4):
            at = last * SPAN + n * 64
            d_ref[a, at : at + 64, :] = parted[a * 64 : (a + 1) * 64, n * 128 : (n + 1) * 128]
    for b in range(4):
        e_ref[b, last * SPAN :, :] = jnp.zeros((SPAN, 128), BF16)

    third = info_ref[UNITS]

    def each_three(turn, carry):
        base = 3 * turn
        odd = third - base

        @pl.when((third >= base) & (third < base + 3))
        def _():
            others = base + jnp.where(odd == 0, 1, 0), base + jnp.where(odd == 2, 1, 2)
            attend_units(d_ref, e_ref, row_ref, ((third, 3), (others[0], 2), (others[1], 2)))

        @pl.when((third < base) | (third >= base + 3))
        def _():
            attend_units(d_ref, e_ref, row_ref, ((base, 2), (base + 1, 2), (base + 2, 2)))

        return carry

    lax.fori_loop(0, UNITS // 3, each_three, 0)

    def join(block, carry):
        base = pl.multiple_of(block * 32, 32)
        rows = jnp.concatenate(
            [
                jnp.concatenate(
                    [
                        e_ref[b, pl.ds(pl.multiple_of((2 * j + i) * SPAN + base, 32), 32), :]
                        for i in range(2)
                        for b in range(4)
                    ],
                    axis=0,
                )
                for j in range(UNITS)
            ],
            axis=1,
        )
        joined = dot(together, rows)
        for j in range(UNITS):
            tile = joined[:, j * 128 : (j + 1) * 128].reshape(32, 2, 4, 128)
            out_ref[pl.ds(base, 32), 2 * j : 2 * j + 2, :, :] = tile.astype(BF16)
        return carry

    lax.fori_loop(0, 8, join, 0, unroll=8)
    rows = jnp.concatenate(
        [
            jnp.concatenate(
                [e_ref[b, last * SPAN + n * 64 : last * SPAN + (n + 1) * 64, :] for b in range(4)],
                axis=0,
            )
            for n in range(4)
        ],
        axis=1,
    )
    joined = dot(together_1, rows)
    for n in range(4):
        tile = joined[:, n * 128 : (n + 1) * 128].reshape(64, 4, 128)
        out_ref[n * 64 : (n + 1) * 64, last, :, :] = tile.astype(BF16)


def home_kernel(codes_ref, home_ref, back_ref, o_ref, dq_ref, dk_ref, dv_ref, rows_ref):
    home = jnp.concatenate([home_ref[...]] * 2, axis=1)[:, :192]

    def rows_of(n, b, count):
        return jnp.concatenate(
            [rows_ref[n, x, pl.ds(b, count, stride=4), :] for x in range(4)], axis=1
        ).astype(BF16)

    for x in range(4):
        rows_ref[1, x, :256, :] = back_ref[:, x, 2 * UNITS, :, :].astype(F32).reshape(256, 128)
    extra = [rows_of(1, b, 64) for b in range(4)]
    for unit in range(UNITS):
        for x in range(4):
            rows_ref[unit % 2, x] = (
                back_ref[:, x, 2 * unit : 2 * unit + 2, :, :].astype(F32).reshape(512, 128)
            )
        picker = jnp.where(home == codes_ref[unit : unit + 1, :192], 1.0, 0.0).astype(BF16)
        for b, ref in enumerate((o_ref, dq_ref, dk_ref, dv_ref)):
            rows = jnp.concatenate([rows_of(unit % 2, b, 128), extra[b]], axis=0)
            total = dot(picker, rows).astype(BF16)
            for x in range(4):
                at = (6 * x + unit) * HD
                ref[:, at : at + HD] = total[:, x * 128 : (x + 1) * 128]


VMEM = pl.BlockSpec(memory_space=pltpu.VMEM)
SMEM = pl.BlockSpec(memory_space=pltpu.SMEM)
SHAPE = jax.ShapeDtypeStruct


def kernel_params():
    return pltpu.CompilerParams(vmem_limit_bytes=40 * MIB)


def pack(me, targets, clips, arrays):
    return pl.pallas_call(
        pack_kernel,
        out_shape=(
            SHAPE((64, 4, PAGES, 4, 128), BF16),
            SHAPE((8, 256), F32),
            SHAPE((128, 128), F32),
            SHAPE((SPAN, 128), jnp.int32),
            SHAPE((8,), jnp.int32),
            SHAPE((1,), jnp.int32),
        ),
        in_specs=[SMEM] + [VMEM] * 6,
        out_specs=(VMEM,) * 4 + (SMEM, SMEM),
        scratch_shapes=[pltpu.VMEM((2, 4, 512, 128), F32)],
        compiler_params=kernel_params(),
    )(me, targets, clips, *arrays)


def label(info, marks):
    return pl.pallas_call(
        label_kernel,
        out_shape=SHAPE((UNITS, 8, 3 * SPAN), F32),
        in_specs=[SMEM, VMEM],
        out_specs=VMEM,
        compiler_params=kernel_params(),
    )(info, marks)


def attend(info, row, came):
    return pl.pallas_call(
        attend_kernel,
        out_shape=SHAPE((SPAN, PAGES, 4, 128), BF16),
        in_specs=[SMEM, VMEM, VMEM],
        out_specs=VMEM,
        scratch_shapes=[
            pltpu.VMEM((4, PAGES * SPAN, 128), BF16),
            pltpu.VMEM((4, PAGES * SPAN, 128), BF16),
        ],
        compiler_params=kernel_params(),
    )(info, row, came)


def unpack(codes, home, back):
    return pl.pallas_call(
        home_kernel,
        out_shape=(SHAPE((128, 24 * HD), BF16),) * 4,
        in_specs=[VMEM] * 3,
        out_specs=(VMEM,) * 4,
        scratch_shapes=[pltpu.VMEM((2, 4, 512, 128), F32)],
        compiler_params=kernel_params(),
    )(codes, home, back)


def body(queries, keys, values, upstream, dest_group, clip_ids):
    group = lax.axis_index("dp")
    device = group * 4 + lax.axis_index("seq")
    targets = dest_group.reshape(SPAN, 128)
    clips = clip_ids.reshape(SPAN, 128)
    me = jnp.stack((device, group)).astype(jnp.int32)
    arrays = (queries, keys, values, upstream)
    send, codes, home, marks, info, heavies = pack(me, targets, clips, arrays)

    def exchange(blocks):
        return lax.all_to_all(blocks, ("dp", "seq"), split_axis=0, concat_axis=0, tiled=True)

    def paged_path():
        came = exchange(send.reshape(SPAN, PAGES, 4, 128))
        back = exchange(attend(info, label(info, marks), came))
        return tuple(unpack(codes, home, back.reshape(64, 4, PAGES, 4, 128)))

    return lax.cond(
        UNITS * heavies.reshape(()) <= 64,
        paged_path,
        lambda: plain_path(queries, keys, values, upstream, dest_group, clip_ids),
    )


def solution(mesh):
    return jax.shard_map(
        body,
        mesh=mesh,
        in_specs=(
            P(("dp", "seq"), None),
            P(("dp", "seq"), None),
            P(("dp", "seq"), None),
            P(("dp", "seq"), None),
            P(),
            P(),
        ),
        out_specs=(
            P(("dp", "seq"), None),
            P(("dp", "seq"), None),
            P(("dp", "seq"), None),
            P(("dp", "seq"), None),
        ),
        check_vma=False,
    )
```

```python
import jax
import jax.numpy as jnp
from jax import lax
from jax.experimental import pallas as pl
from jax.experimental.pallas import tpu as pltpu
from jax.sharding import PartitionSpec as P

HD = 128


def prior_count(targets):
    length = targets.shape[-1]
    earlier = lax.broadcasted_iota(jnp.int32, (length, length), 1) < lax.broadcasted_iota(
        jnp.int32, (length, length), 0
    )
    matching = targets[..., :, None] == targets[..., None, :]
    return jnp.sum((matching & earlier).astype(jnp.int32), axis=-1)


def slot_labels(targets, clip_table, group_index, capacity):
    arriving = targets == group_index
    row_ranks = prior_count(targets)
    slot_ids = lax.broadcasted_iota(jnp.int32, (capacity,), 0)
    filled = arriving[:, None, :] & (row_ranks[:, None, :] == slot_ids[None, :, None])
    return jnp.sum(jnp.where(filled, clip_table[:, None, :] + 1, 0), axis=-1)


def return_rows(positions, slot_count, stacked):
    picker = (
        positions[:, None] == lax.broadcasted_iota(jnp.int32, (positions.shape[0], slot_count), 1)
    ).astype(jnp.bfloat16)
    return jnp.einsum("ts,nsc->ntc", picker, stacked, preferred_element_type=jnp.float32).astype(
        jnp.bfloat16
    )


def attend_forward(query_rows, key_rows, value_rows, related):
    scale = HD ** (-0.5)
    contract_cols = (((1,), (1,)), ((), ()))
    prob_list, probs_b_list, out_list = ([], [], [])
    for head_index in range(query_rows.shape[1] // HD):
        lower = head_index * HD
        query_head = query_rows[:, lower : lower + HD]
        key_head = key_rows[:, lower : lower + HD]
        value_head = value_rows[:, lower : lower + HD]
        scores = (
            lax.dot_general(query_head, key_head, contract_cols, preferred_element_type=jnp.float32)
            * scale
        )
        scores = jnp.where(related, scores, -1e30)
        row_max = jnp.max(scores, axis=1, keepdims=True)
        weights = jnp.where(related, jnp.exp(scores - row_max), 0.0)
        probs = weights / jnp.sum(weights, axis=1, keepdims=True)
        probs_b = probs.astype(jnp.bfloat16)
        prob_list.append(probs)
        probs_b_list.append(probs_b)
        out_list.append(
            jnp.dot(probs_b, value_head, preferred_element_type=jnp.float32).astype(jnp.bfloat16)
        )
    return (prob_list, probs_b_list, jnp.concatenate(out_list, axis=1))


def attend_backward(
    query_rows, key_rows, value_rows, upstream_rows, attended, prob_list, probs_b_list
):
    scale = HD ** (-0.5)
    contract_cols = (((1,), (1,)), ((), ()))
    contract_rows = (((0,), (0,)), ((), ()))
    query_grads, key_grads, value_grads = ([], [], [])
    for head_index in range(query_rows.shape[1] // HD):
        lower = head_index * HD
        query_head = query_rows[:, lower : lower + HD]
        key_head = key_rows[:, lower : lower + HD]
        value_head = value_rows[:, lower : lower + HD]
        upstream_head = upstream_rows[:, lower : lower + HD]
        out_head = attended[:, lower : lower + HD]
        delta = jnp.sum(
            upstream_head.astype(jnp.float32) * out_head.astype(jnp.float32), axis=1, keepdims=True
        )
        dprobs = lax.dot_general(
            upstream_head, value_head, contract_cols, preferred_element_type=jnp.float32
        )
        dscores = (prob_list[head_index] * (dprobs - delta)).astype(jnp.bfloat16)
        query_grads.append(
            (jnp.dot(dscores, key_head, preferred_element_type=jnp.float32) * scale).astype(
                jnp.bfloat16
            )
        )
        key_grads.append(
            (
                lax.dot_general(
                    dscores, query_head, contract_rows, preferred_element_type=jnp.float32
                )
                * scale
            ).astype(jnp.bfloat16)
        )
        value_grads.append(
            lax.dot_general(
                probs_b_list[head_index],
                upstream_head,
                contract_rows,
                preferred_element_type=jnp.float32,
            ).astype(jnp.bfloat16)
        )
    return (
        jnp.concatenate(query_grads, axis=1),
        jnp.concatenate(key_grads, axis=1),
        jnp.concatenate(value_grads, axis=1),
    )


def plain_path(queries, keys, values, upstream, dest_group, clip_ids):
    group_count = lax.axis_size("dp")
    part_count = lax.axis_size("seq")
    group_index = lax.axis_index("dp")
    seq_index = lax.axis_index("seq")
    row_count = queries.shape[0]
    capacity = (3 * row_count + 2 * group_count - 1) // (2 * group_count)
    targets = dest_group[:, 0].reshape(group_count, part_count, row_count)
    clip_table = clip_ids.reshape(group_count, part_count, row_count)
    label_table = slot_labels(
        targets.reshape(group_count * part_count, row_count),
        clip_table.reshape(group_count * part_count, row_count),
        group_index,
        capacity,
    ).reshape(group_count, part_count, capacity)
    own_group = lax.dynamic_index_in_dim(targets, group_index, 0, keepdims=False)
    labels = label_table.reshape(-1)
    own_rows = lax.dynamic_index_in_dim(own_group, seq_index, 0, keepdims=False)
    positions = own_rows * capacity + prior_count(own_rows)
    slots = group_count * capacity
    picker = (
        lax.broadcasted_iota(jnp.int32, (slots, row_count), 0) == positions[None, :]
    ).astype(jnp.bfloat16)
    width = queries.shape[1] // part_count
    stacked = jnp.stack((queries, keys, values, upstream))
    packed = jnp.einsum("st,ntc->snc", picker, stacked, preferred_element_type=jnp.float32).astype(
        jnp.bfloat16
    )
    blocks = packed.reshape(group_count, capacity, 4, part_count, width)
    blocks = jnp.transpose(blocks, (0, 3, 1, 2, 4)).reshape(-1, capacity, 4, width)
    arrived = lax.all_to_all(blocks, ("dp", "seq"), split_axis=0, concat_axis=0, tiled=True)
    regrouped = jnp.transpose(arrived, (2, 0, 1, 3)).reshape(4, -1, width)
    slot_total = labels.shape[0]
    identity = lax.broadcasted_iota(jnp.int32, (slot_total, slot_total), 0) == lax.broadcasted_iota(
        jnp.int32, (slot_total, slot_total), 1
    )
    related = (labels[:, None] == labels[None, :]) & (labels[:, None] > 0) | identity
    prob_list, probs_b_list, attended = attend_forward(
        regrouped[0], regrouped[1], regrouped[2], related
    )
    gradients = attend_backward(
        regrouped[0], regrouped[1], regrouped[2], regrouped[3], attended, prob_list, probs_b_list
    )
    results = jnp.stack((attended, gradients[0], gradients[1], gradients[2]), axis=1)
    results = results.reshape(-1, capacity, 4, width)
    routed_back = lax.all_to_all(results, ("dp", "seq"), split_axis=0, concat_axis=0, tiled=True)
    routed_back = routed_back.reshape(group_count, part_count, capacity, 4, width)
    routed_back = jnp.transpose(routed_back, (3, 0, 2, 1, 4)).reshape(4, slots, -1)
    all_home = return_rows(positions, slots, routed_back)
    return (all_home[0], all_home[1], all_home[2], all_home[3])

UNITS = 6
PAGES = 13
TRADES = UNITS - 1
SPAN = 256
MIB = 1 << 20
F32 = jnp.float32
BF16 = jnp.bfloat16
ROWS_T = (((1,), (1,)), ((), ()))
COLS_T = (((0,), (0,)), ((), ()))


def iota(shape, dim):
    return lax.broadcasted_iota(jnp.int32, shape, dim)


def dot(a, b, dims=(((1,), (0,)), ((), ()))):
    return lax.dot_general(a, b, dims, preferred_element_type=F32)


def unit_table(heavy, heavy_rank):
    square = (128, 128)
    group, lane = iota(square, 0), iota(square, 1)

    def total(cond, values):
        return jnp.sum(jnp.where(cond, values, 0.0), axis=1, keepdims=True).astype(jnp.int32)

    heavy_rank = heavy_rank.astype(jnp.int32)
    lane_f = lane.astype(F32)
    is_heavy = total(lane == group, heavy) > 0
    below = total(lane < group, heavy)
    heavies = total(lane >= 0, heavy)
    rank = group[:, :1] - below
    light = (lane < 64) & (heavy < 0.5)
    trades = jnp.logical_not(is_heavy) & (rank < TRADES * heavies)
    turn = (rank * 13) >> 6
    served = total((heavy > 0.5) & (heavy_rank == turn), lane_f)
    third = jnp.where(is_heavy, 0, jnp.where(trades, rank - TRADES * turn + 1, -1))
    table = jnp.zeros(square, jnp.int32)
    for unit in range(UNITS):
        source = group[:, :1]
        if unit > 0:
            light_rank = lane - heavy_rank
            traded = total(light & (light_rank == TRADES * below + unit - 1), lane_f)
            source = jnp.where(is_heavy, traded, jnp.where(third == unit, served, source))
        table = jnp.where(lane == unit, source, table)
        table = jnp.where(lane == UNITS + unit, jnp.where(third == unit, 3 * source + 2, -1), table)
    return jnp.where(lane == 2 * UNITS, third, table), heavies


def pack_kernel(
    me_ref,
    targets_ref,
    clips_ref,
    q_ref,
    k_ref,
    v_ref,
    u_ref,
    send_ref,
    codes_ref,
    home_ref,
    marks_ref,
    info_ref,
    heavies_ref,
    rows_ref,
):
    device, group = me_ref[0], me_ref[1]
    targets = targets_ref[...]
    marks_ref[...] = 4 * targets + clips_ref[...] + 1
    lane = iota((SPAN, 128), 1)
    ones = jnp.ones((128, 128), BF16)
    flags = jnp.zeros((SPAN, 128), jnp.int32)
    shift = 2 * (lane & 7)
    spread = jnp.left_shift(jnp.ones((SPAN, 128), jnp.int32), 2 * (targets & 7))
    for word in range(8):
        bits = jnp.where((targets >> 3) == word, spread, 0).astype(F32).astype(BF16)
        counts = dot(bits, ones).astype(jnp.int32)
        three = jnp.right_shift(counts, shift) & jnp.right_shift(counts, shift + 1) & 1
        flags = jnp.where((lane >> 3) == word, three, flags)
    heavy = jnp.max(flags.astype(F32), axis=0, keepdims=True)
    square = (128, 128)
    row, col = iota(square, 0), iota(square, 1)
    heavy = jnp.broadcast_to(heavy, square)
    earlier = jnp.where(row < col, 1.0, 0.0).astype(BF16)
    table, heavies = unit_table(heavy, dot(heavy.astype(BF16), earlier))

    table_f = table.astype(F32)
    table_t = table_f.T
    twice_c = jnp.where(row >> 1 == col, 1.0, 0.0).astype(BF16)
    twice_l = jnp.where(col >> 1 == row, 1.0, 0.0).astype(BF16)
    pages_c = 3.0 * dot(twice_c, table_f.astype(BF16)) + (row & 1).astype(F32)
    pages_l = 3.0 * dot(table_t[:8].astype(BF16), twice_l) + (col[:8] & 1).astype(F32)
    codes_ref[:, :128] = pages_l
    codes_ref[:, 128:] = table_t[UNITS : UNITS + 8]

    mine = jnp.broadcast_to(targets_ref[pl.ds(device, 1), :].astype(F32), square)
    mine_c = mine.T
    same = mine == mine_c
    prior_l = jnp.sum(jnp.where(same & (row < col), 1.0, 0.0), axis=0, keepdims=True)
    prior_c = jnp.sum(jnp.where(same & (col < row), 1.0, 0.0), axis=1, keepdims=True)
    key_l = 3.0 * mine[:1] + prior_l
    home_ref[...] = 3.0 * mine_c + prior_c

    extra = [None] * 4
    for unit in range(UNITS):
        wanted = jnp.concatenate(
            [pages_c[:, unit : unit + 1], table_f[:64, UNITS + unit : UNITS + unit + 1]], axis=0
        )
        picker = jnp.where(wanted == key_l, 1.0, 0.0).astype(BF16)
        for a, ref in enumerate((q_ref, k_ref, v_ref, u_ref)):
            columns = jnp.concatenate(
                [ref[:, (6 * x + unit) * HD : (6 * x + unit + 1) * HD] for x in range(4)], axis=1
            )
            picked = dot(picker, columns)
            extra[a] = picked[128:] if unit == 0 else extra[a] + picked[128:]
            for x in range(4):
                rows_ref[unit % 2, x, pl.ds(a, 128, stride=4), :] = picked[
                    :128, x * 128 : (x + 1) * 128
                ]
        for x in range(4):
            tile = rows_ref[unit % 2, x].reshape(64, 2, 4, 128)
            send_ref[:, x, 2 * unit : 2 * unit + 2, :, :] = tile.astype(BF16)
    for x in range(4):
        for a in range(4):
            rows_ref[0, x, pl.ds(a, 64, stride=4), :] = extra[a][:, x * 128 : (x + 1) * 128]
        tile = rows_ref[0, x, :256, :].reshape(64, 4, 128)
        send_ref[:, x, 2 * UNITS, :, :] = tile.astype(BF16)

    own = jnp.sum(jnp.where(row == group, table_f, 0.0), axis=0, keepdims=True)
    for unit in range(UNITS):
        info_ref[unit] = jnp.sum(jnp.where(col[:1] == unit, own, 0.0)).astype(jnp.int32)
    info_ref[UNITS] = jnp.sum(jnp.where(col[:1] == 2 * UNITS, own, 0.0)).astype(jnp.int32)
    heavies_ref[0] = jnp.sum(heavy[:1]).astype(jnp.int32)


def label_kernel(info_ref, marks_ref, row_ref):
    targets = marks_ref[...] >> 2
    clips = marks_ref[...] & 3
    row, col = iota((128, 128), 0), iota((128, 128), 1)
    earlier = jnp.where(row < col, 1.0, 0.0).astype(BF16)
    ones = jnp.ones((128, 128), BF16)
    for unit in range(UNITS):
        arriving = targets == info_ref[unit]
        rank = dot(jnp.where(arriving, 1.0, 0.0).astype(BF16), earlier).astype(jnp.int32)
        for slot in range(3):
            labels = jnp.where(arriving & (rank == slot), clips, 0).astype(F32).astype(BF16)
            row_ref[unit, :, slot * SPAN : (slot + 1) * SPAN] = dot(ones[:8], labels, ROWS_T)


def attend_units(d_ref, e_ref, row_ref, units):
    scale = HD**-0.5
    everything = []
    for unit, count in units:
        start = pl.multiple_of(unit * (2 * SPAN), 2 * SPAN)
        spans = [(start, 2 * SPAN)] + ([(2 * UNITS * SPAN, SPAN)] if count == 3 else [])

        def load(a, spans=spans):
            parts = [d_ref[a, pl.ds(place, size), :] for place, size in spans]
            return parts[0] if len(parts) == 1 else jnp.concatenate(parts, axis=0)

        labels = row_ref[unit, :, : count * SPAN]
        first = jnp.where(iota((8, 128), 0) == 0, 1.0, 0.0).astype(BF16)
        column = dot(labels.astype(BF16), first, COLS_T)
        related = jnp.concatenate([column] * (2 * count), axis=1) == labels[:1]
        query, key, value, cotangent = load(0), load(1), load(2), load(3)
        scores = dot(query, key, ROWS_T)
        dprobs = dot(cotangent, value, ROWS_T)
        everything.append([spans, query, key, value, cotangent, related, scores, dprobs])
    for state in everything:
        related, scores = state[5], state[6]
        scores = jnp.where(related, scores, -1e30)
        top = jnp.max(scores, axis=1, keepdims=True)
        weights = jnp.exp2((scores - top) * (scale * 1.4426950408889634))
        probs = weights * (1.0 / jnp.sum(weights, axis=1, keepdims=True))
        state += [probs, probs.astype(BF16)]
    for spans, query, key, value, cotangent, related, scores, dprobs, probs, probs_b in everything:
        attended = dot(probs_b, value).astype(BF16)
        delta = jnp.sum(cotangent.astype(F32) * attended.astype(F32), axis=1, keepdims=True)
        dscores = (probs * (dprobs - delta)).astype(BF16)
        results = (
            attended,
            (dot(dscores, key) * scale).astype(BF16),
            (dot(query, dscores, COLS_T) * scale).T.astype(BF16),
            dot(cotangent, probs_b, COLS_T).T.astype(BF16),
        )
        for b, result in enumerate(results):
            at = 0
            for place, size in spans:
                e_ref[b, pl.ds(place, size), :] = result[at : at + size]
                at += size


def attend_kernel(info_ref, row_ref, came_ref, out_ref, d_ref, e_ref):
    row, col = iota((SPAN, SPAN), 0), iota((SPAN, SPAN), 1)
    apart = jnp.where(((row & 31) << 3) + (row >> 5) == col, 1.0, 0.0).astype(BF16)
    together = jnp.where(((col & 31) << 3) + (col >> 5) == row, 1.0, 0.0).astype(BF16)
    apart_1 = jnp.where(((row & 63) << 2) + (row >> 6) == col, 1.0, 0.0).astype(BF16)
    together_1 = jnp.where(((col & 63) << 2) + (col >> 6) == row, 1.0, 0.0).astype(BF16)
    last = 2 * UNITS

    def split(block, carry):
        base = pl.multiple_of(block * 32, 32)
        rows = jnp.concatenate(
            [
                came_ref[pl.ds(base, 32), 2 * j : 2 * j + 2, :, :].astype(F32).reshape(SPAN, 128)
                for j in range(UNITS)
            ],
            axis=1,
        ).astype(BF16)
        parted = dot(apart, rows).astype(BF16)
        for j in range(UNITS):
            for i in range(2):
                for a in range(4):
                    at = (4 * i + a) * 32
                    d_ref[a, pl.ds(pl.multiple_of((2 * j + i) * SPAN + base, 32), 32), :] = parted[
                        at : at + 32, j * 128 : (j + 1) * 128
                    ]
        return carry

    lax.fori_loop(0, 8, split, 0, unroll=8)
    rows = jnp.concatenate(
        [
            came_ref[n * 64 : (n + 1) * 64, last, :, :].astype(F32).reshape(SPAN, 128)
            for n in range(4)
        ],
        axis=1,
    ).astype(BF16)
    parted = dot(apart_1, rows).astype(BF16)
    for n in range(4):
        for a in range(4):
            at = last * SPAN + n * 64
            d_ref[a, at : at + 64, :] = parted[a * 64 : (a + 1) * 64, n * 128 : (n + 1) * 128]
    for b in range(4):
        e_ref[b, last * SPAN :, :] = jnp.zeros((SPAN, 128), BF16)

    third = info_ref[UNITS]

    def each_pair(pair, carry):
        @pl.when(pair == third >> 1)
        def _():
            attend_units(d_ref, e_ref, row_ref, ((third, 3), (third ^ 1, 2)))

        @pl.when(pair != third >> 1)
        def _():
            attend_units(d_ref, e_ref, row_ref, ((2 * pair, 2), (2 * pair + 1, 2)))

        return carry

    lax.fori_loop(0, UNITS // 2, each_pair, 0)

    def join(block, carry):
        base = pl.multiple_of(block * 32, 32)
        rows = jnp.concatenate(
            [
                jnp.concatenate(
                    [
                        e_ref[b, pl.ds(pl.multiple_of((2 * j + i) * SPAN + base, 32), 32), :]
                        for i in range(2)
                        for b in range(4)
                    ],
                    axis=0,
                )
                for j in range(UNITS)
            ],
            axis=1,
        )
        joined = dot(together, rows)
        for j in range(UNITS):
            tile = joined[:, j * 128 : (j + 1) * 128].reshape(32, 2, 4, 128)
            out_ref[pl.ds(base, 32), 2 * j : 2 * j + 2, :, :] = tile.astype(BF16)
        return carry

    lax.fori_loop(0, 8, join, 0, unroll=8)
    rows = jnp.concatenate(
        [
            jnp.concatenate(
                [e_ref[b, last * SPAN + n * 64 : last * SPAN + (n + 1) * 64, :] for b in range(4)],
                axis=0,
            )
            for n in range(4)
        ],
        axis=1,
    )
    joined = dot(together_1, rows)
    for n in range(4):
        tile = joined[:, n * 128 : (n + 1) * 128].reshape(64, 4, 128)
        out_ref[n * 64 : (n + 1) * 64, last, :, :] = tile.astype(BF16)


def home_kernel(codes_ref, home_ref, back_ref, o_ref, dq_ref, dk_ref, dv_ref, rows_ref):
    home = jnp.concatenate([home_ref[...]] * 2, axis=1)[:, :192]

    def rows_of(n, b, count):
        return jnp.concatenate(
            [rows_ref[n, x, pl.ds(b, count, stride=4), :] for x in range(4)], axis=1
        ).astype(BF16)

    for x in range(4):
        rows_ref[1, x, :256, :] = back_ref[:, x, 2 * UNITS, :, :].astype(F32).reshape(256, 128)
    extra = [rows_of(1, b, 64) for b in range(4)]
    for unit in range(UNITS):
        for x in range(4):
            rows_ref[unit % 2, x] = (
                back_ref[:, x, 2 * unit : 2 * unit + 2, :, :].astype(F32).reshape(512, 128)
            )
        picker = jnp.where(home == codes_ref[unit : unit + 1, :192], 1.0, 0.0).astype(BF16)
        for b, ref in enumerate((o_ref, dq_ref, dk_ref, dv_ref)):
            rows = jnp.concatenate([rows_of(unit % 2, b, 128), extra[b]], axis=0)
            total = dot(picker, rows).astype(BF16)
            for x in range(4):
                at = (6 * x + unit) * HD
                ref[:, at : at + HD] = total[:, x * 128 : (x + 1) * 128]


VMEM = pl.BlockSpec(memory_space=pltpu.VMEM)
SMEM = pl.BlockSpec(memory_space=pltpu.SMEM)
SHAPE = jax.ShapeDtypeStruct


def kernel_params():
    return pltpu.CompilerParams(vmem_limit_bytes=40 * MIB)


def pack(me, targets, clips, arrays):
    return pl.pallas_call(
        pack_kernel,
        out_shape=(
            SHAPE((64, 4, PAGES, 4, 128), BF16),
            SHAPE((8, 256), F32),
            SHAPE((128, 128), F32),
            SHAPE((SPAN, 128), jnp.int32),
            SHAPE((8,), jnp.int32),
            SHAPE((1,), jnp.int32),
        ),
        in_specs=[SMEM] + [VMEM] * 6,
        out_specs=(VMEM,) * 4 + (SMEM, SMEM),
        scratch_shapes=[pltpu.VMEM((2, 4, 512, 128), F32)],
        compiler_params=kernel_params(),
    )(me, targets, clips, *arrays)


def label(info, marks):
    return pl.pallas_call(
        label_kernel,
        out_shape=SHAPE((UNITS, 8, 3 * SPAN), F32),
        in_specs=[SMEM, VMEM],
        out_specs=VMEM,
        compiler_params=kernel_params(),
    )(info, marks)


def attend(info, row, came):
    return pl.pallas_call(
        attend_kernel,
        out_shape=SHAPE((SPAN, PAGES, 4, 128), BF16),
        in_specs=[SMEM, VMEM, VMEM],
        out_specs=VMEM,
        scratch_shapes=[
            pltpu.VMEM((4, PAGES * SPAN, 128), BF16),
            pltpu.VMEM((4, PAGES * SPAN, 128), BF16),
        ],
        compiler_params=kernel_params(),
    )(info, row, came)


def unpack(codes, home, back):
    return pl.pallas_call(
        home_kernel,
        out_shape=(SHAPE((128, 24 * HD), BF16),) * 4,
        in_specs=[VMEM] * 3,
        out_specs=(VMEM,) * 4,
        scratch_shapes=[pltpu.VMEM((2, 4, 512, 128), F32)],
        compiler_params=kernel_params(),
    )(codes, home, back)


def body(queries, keys, values, upstream, dest_group, clip_ids):
    group = lax.axis_index("dp")
    device = group * 4 + lax.axis_index("seq")
    targets = dest_group.reshape(SPAN, 128)
    clips = clip_ids.reshape(SPAN, 128)
    me = jnp.stack((device, group)).astype(jnp.int32)
    arrays = (queries, keys, values, upstream)
    send, codes, home, marks, info, heavies = pack(me, targets, clips, arrays)

    def exchange(blocks):
        return lax.all_to_all(blocks, ("dp", "seq"), split_axis=0, concat_axis=0, tiled=True)

    def paged_path():
        came = exchange(send.reshape(SPAN, PAGES, 4, 128))
        back = exchange(attend(info, label(info, marks), came))
        return tuple(unpack(codes, home, back.reshape(64, 4, PAGES, 4, 128)))

    return lax.cond(
        UNITS * heavies.reshape(()) <= 64,
        paged_path,
        lambda: plain_path(queries, keys, values, upstream, dest_group, clip_ids),
    )


def solution(mesh):
    return jax.shard_map(
        body,
        mesh=mesh,
        in_specs=(
            P(("dp", "seq"), None),
            P(("dp", "seq"), None),
            P(("dp", "seq"), None),
            P(("dp", "seq"), None),
            P(),
            P(),
        ),
        out_specs=(
            P(("dp", "seq"), None),
            P(("dp", "seq"), None),
            P(("dp", "seq"), None),
            P(("dp", "seq"), None),
        ),
        check_vma=False,
    )
```
